256 devices in a mesh: gx: 64 (over z, y, core), gy: 4 (over x).
Axes of the slice: x: 4, y: 4, z: 8, core: 2. Of those that a mesh axis runs over, the one named last changes fastest.
Arguments:
- hamiltonian: float32 [64, 4, 4, 64, 512], P('gx', 'gy')
- intersection: float32 [64, 4, 4, 64, 512], P('gx', 'gy')
- density: float32 [64, 4, 4, 64, 512], P('gx', 'gy')
- leaving: int32 [64, 4, 4, 1], P('gx', 'gy'), may hold values from 0 to 3, as said below
- code_ids: int32 [64, 4, 4, 8], P('gx', 'gy'), may hold values from 0 to 8, as said below
- slot_ids: int32 [64, 4, 4, 8], P('gx', 'gy'), may hold values from 0 to 3, as said below
Outputs:
- purified: float32 [64, 4, 4, 64, 512], P('gx', 'gy')
- energy: float32 [], replicated
The draws below stay inside these ranges and needn't reach their ends.
Inputs may be any that keep to these rules, and one draw needn't show every extreme that they name: `leaving`: the slots listed for one device are all different. `code_ids`: the first entry of every block row is code 4 with the row's own slot; the 8 (code, slot) pairs of a row are all different. `slot_ids`: paired with code_ids as stated there.
All inputs are finite; a program needn't handle non-finite values.
Results may differ from the reference program's by a relative error of at most 0.0003.
Values sent between devices are 32-bit elements; how exact they have to be, the bound alone decides.
A program may use at most 128 MiB of HBM per device.

```python
import jax
import jax.numpy as jnp
from jax import lax

BLOCK = 64
KEPT = 8
GROUPS = 4
MOVING = 1
ITERS = 2
SLABS = 64
STRIPS = 4
COLUMNS = 512
BASIS = 65536


def block_matrix(key, noise_scale, diag_lo, diag_hi):
    first, second = jax.random.split(key)
    shape = (SLABS, STRIPS, GROUPS, BLOCK, COLUMNS)
    noise = noise_scale * jax.random.normal(first, shape, jnp.float32)
    diagonal = jax.random.uniform(second, (SLABS, STRIPS, GROUPS, BLOCK), jnp.float32, diag_lo, diag_hi)
    identity = (jnp.arange(COLUMNS)[None, :] == jnp.arange(BLOCK)[:, None]).astype(jnp.float32)
    return noise + diagonal[..., None] * identity


def draw_hamiltonian(key, part):
    key = jax.random.fold_in(key, 1)
    return block_matrix(key, 0.05, -1.5, 0.5)


def draw_intersection(key, part):
    key = jax.random.fold_in(key, 2)
    return block_matrix(key, 0.05, 0.9, 1.1)


def draw_density(key, part):
    key = jax.random.fold_in(key, 3)
    return block_matrix(key, 0.05, 0.2, 0.8)


def draw_leaving(key, part):
    key = jax.random.fold_in(key, 4)
    scores = jax.random.randint(key, (SLABS, STRIPS, GROUPS), 0, 1 << 20) * GROUPS + jnp.arange(GROUPS, dtype=jnp.int32)
    order = jnp.argsort(scores, axis=-1).astype(jnp.int32)
    return order[..., :4 * MOVING].reshape(SLABS, STRIPS, 4, MOVING)


def pattern_pair(key):
    key = jax.random.fold_in(key, 7)
    total = 9 * GROUPS
    candidate = jnp.arange(total, dtype=jnp.int32)
    own = 4 * GROUPS + jnp.arange(GROUPS, dtype=jnp.int32)
    scores = jax.random.randint(key, (SLABS, STRIPS, GROUPS, total), 0, 1 << 20) * total + candidate
    scores = jnp.where(candidate[None, :] == own[:, None], -1, scores)
    picked = lax.top_k(scores, KEPT - 1)[1].astype(jnp.int32)
    own_full = jnp.broadcast_to(own[:, None], (SLABS, STRIPS, GROUPS, 1))
    whole = jnp.concatenate([own_full, picked], axis=-1)
    return (whole // GROUPS, whole % GROUPS)


def draw_code_ids(key, part):
    return pattern_pair(key)[0]


def draw_slot_ids(key, part):
    return pattern_pair(key)[1]


def setup_inputs(seed: int = 0) -> dict:
    arg_keys = jax.random.split(jax.random.key(seed), 7)
    hamiltonian = draw_hamiltonian(jax.random.fold_in(arg_keys[6], 71), 0)
    intersection = draw_intersection(jax.random.fold_in(arg_keys[6], 71), 0)
    density = draw_density(jax.random.fold_in(arg_keys[6], 71), 0)
    leaving = draw_leaving(jax.random.fold_in(arg_keys[6], 71), 0)
    code_ids = draw_code_ids(jax.random.fold_in(arg_keys[6], 71), 0)
    slot_ids = draw_slot_ids(jax.random.fold_in(arg_keys[6], 71), 0)
    return dict(hamiltonian=hamiltonian, intersection=intersection, density=density, leaving=leaving, code_ids=code_ids, slot_ids=slot_ids)


def local_product(left_rows, rim_rows, code_list, slot_list, rim_codes, rim_slots):
    groups, width, columns = left_rows.shape
    kept = code_list.shape[1]
    row_index = (code_list * groups + slot_list).astype(jnp.int32)
    next_codes = jnp.take(rim_codes.reshape(9 * groups, kept), row_index, axis=0)
    next_slots = jnp.take(rim_slots.reshape(9 * groups, kept), row_index, axis=0)
    left_dx = code_list // 3 - 1
    left_dy = code_list % 3 - 1
    next_dx = next_codes // 3 - 1
    next_dy = next_codes % 3 - 1
    same_x = (left_dx[:, :, None, None] + next_dx[:, :, None, :]) == left_dx[:, None, :, None]
    same_y = (left_dy[:, :, None, None] + next_dy[:, :, None, :]) == left_dy[:, None, :, None]
    same_slot = next_slots[:, :, None, :] == slot_list[:, None, :, None]
    matches = (same_x & same_y & same_slot).astype(jnp.float32)
    gathered = jnp.take(rim_rows.reshape(9 * groups, width, columns), row_index.reshape(-1), axis=0)
    gathered = gathered.reshape(groups, kept, width, kept, width)
    partial_rows = jnp.einsum('ipar,iarcq->iapcq', left_rows.reshape(groups, width, kept, width), gathered, precision=lax.Precision.HIGHEST)
    result = jnp.einsum('iabc,iapcq->ipbq', matches, partial_rows, precision=lax.Precision.HIGHEST)
    return result.reshape(groups, width, kept * width)


def product(left_all, right_all, code_ids, slot_ids):
    devices = SLABS * STRIPS
    left_flat = left_all.reshape((devices,) + left_all.shape[2:])
    right_flat = right_all.reshape((devices,) + right_all.shape[2:])
    code_flat = code_ids.reshape((devices,) + code_ids.shape[2:])
    slot_flat = slot_ids.reshape((devices,) + slot_ids.shape[2:])
    offsets = jnp.arange(9, dtype=jnp.int32)
    shift_x = offsets // 3 - 1
    shift_y = offsets % 3 - 1

    def one_device(device):
        pos_x = device // STRIPS
        pos_y = device % STRIPS
        beside = (((pos_x + shift_x) % SLABS) * STRIPS + (pos_y + shift_y) % STRIPS).astype(jnp.int32)
        return local_product(left_flat[device], jnp.take(right_flat, beside, axis=0), code_flat[device], slot_flat[device], jnp.take(code_flat, beside, axis=0), jnp.take(slot_flat, beside, axis=0))

    result = lax.map(one_device, jnp.arange(devices, dtype=jnp.int32))
    return result.reshape(left_all.shape)


def reference(hamiltonian, intersection, density, leaving, code_ids, slot_ids):
    stacked = jnp.stack([hamiltonian, intersection, density], axis=2)

    def outgoing(face):
        chosen_slots = leaving[:, :, face, :]
        return jnp.take_along_axis(stacked, chosen_slots[:, :, None, :, None, None], axis=3)

    arrive = jnp.concatenate([jnp.roll(outgoing(0), 1, axis=0), jnp.roll(outgoing(1), -1, axis=0), jnp.roll(outgoing(2), 1, axis=1), jnp.roll(outgoing(3), -1, axis=1)], axis=3)
    landing = jnp.concatenate([leaving[:, :, 1, :], leaving[:, :, 0, :], leaving[:, :, 3, :], leaving[:, :, 2, :]], axis=2)

    def place(rows_here, slots_here, arrive_here):
        return rows_here.at[:, slots_here].set(arrive_here)

    stacked = jax.vmap(jax.vmap(place))(stacked, landing, arrive)
    ham_rows = stacked[:, :, 0]
    ovl_rows = stacked[:, :, 1]
    den_rows = stacked[:, :, 2]
    count_start = jnp.sum(den_rows * ovl_rows)
    for step in range(ITERS):
        first = product(den_rows, ovl_rows, code_ids, slot_ids)
        second = product(first, den_rows, code_ids, slot_ids)
        third = product(second, ovl_rows, code_ids, slot_ids)
        fourth = product(third, den_rows, code_ids, slot_ids)
        mixed = 3.0 * second - 2.0 * fourth
        count_now = jnp.sum(mixed * ovl_rows)
        den_rows = (count_start / count_now) * mixed
    energy = jnp.sum(den_rows * ham_rows) / jnp.float32(BASIS)
    return den_rows, energy
```

```python
import functools

import jax
import jax.numpy as jnp
from jax import lax
from jax.experimental import pallas as pl
from jax.experimental.pallas import tpu as pltpu
from jax.sharding import PartitionSpec as P

MESH = pl.DeviceIdType.MESH
F32, BF16, I32 = jnp.float32, jnp.bfloat16, jnp.int32
A, B, C, D = range(4)
SIDE, KEPT, TYPES = 64, 8, 4
COLUMNS = SIDE * KEPT
OVL, DEN, MIX = range(3)
BEHIND = (1, 0, 3, 2)
AROUND = [(ux, uy) for ux in (-1, 0, 1) for uy in (-1, 0, 1) if (ux, uy) != (0, 0)]
LOW = 4


def row_id(dx, dy, kind):
    return (3 * (dx + 1) + (dy + 1)) * TYPES + kind


def domain_key(code):
    across = (code * 11) >> 5
    return (across - 1) * 64 + (code - 3 * across - 1) * 8


def folded(tile):
    return jnp.sum(tile.reshape(tile.shape[0] // 8, 8, 128), axis=0)


def kernel(
    nx, ny,
    ham, ovl, den, leaving, codes, slots,
    out, energy,
    rim, ham_out, ham_home, tiles_s, tiles_p, lhs, second, last,
    near, near_s, index_v, index_s, near_sums, far_sums,
    send_sem, recv_sem, ham_send, ham_recv, near_send, near_recv, sum_send, sum_recv, local_sem,
):
    x, y = lax.axis_index("gx"), lax.axis_index("gy")
    high = nx // LOW
    group = LOW * ny
    at_high, at_low = x // LOW, (x % LOW) * ny + y

    def beside(ux, uy):
        return (lax.rem(x + ux + nx, nx), lax.rem(y + uy + ny, ny))

    def near_peer(j):
        return (at_high * LOW + j // ny, j % ny)

    def far_peer(j):
        return (j * LOW + x % LOW, y)

    barrier = pltpu.get_barrier_semaphore()
    for ux, uy in AROUND:
        pl.semaphore_signal(barrier, inc=1, device_id=beside(ux, uy), device_id_type=MESH)

    def greet_near(o, carry):
        pl.semaphore_signal(barrier, inc=1, device_id=near_peer((at_low + o) % group), device_id_type=MESH)
        return carry

    def greet_far(o, carry):
        pl.semaphore_signal(barrier, inc=1, device_id=far_peer((at_high + o) % high), device_id_type=MESH)
        return carry

    lax.fori_loop(1, group, greet_near, 0)
    lax.fori_loop(1, high, greet_far, 0)

    lane = lax.broadcasted_iota(I32, (8, 128), 1)
    sub = lax.broadcasted_iota(I32, (8, 128), 0)

    start = jnp.zeros((8, 128), F32)
    for kind in range(TYPES):
        slot = leaving[kind]
        mine = row_id(*((1, 0), (-1, 0), (0, 1), (0, -1))[kind], kind)
        s_row, p_row = ovl[0, 0, slot], den[0, 0, slot]
        rim[OVL, mine] = s_row
        rim[DEN, mine] = p_row
        prod = s_row * p_row
        for k in range(COLUMNS // 128):
            start += folded(prod[:, k * 128 : (k + 1) * 128])

    note = jnp.zeros((8, 128), I32)
    for kind in range(TYPES):
        slot = leaving[BEHIND[kind]]
        for c in range(KEPT):
            key = domain_key(codes[slot, c]) + slots[slot, c]
            note = jnp.where((sub == kind) & (lane == c), key, note)
        note = jnp.where((sub == TYPES) & (lane == slot), kind, note)
    near[4] = note

    pl.semaphore_wait(barrier, len(AROUND) + group - 1 + high - 1)

    def row_copy(m, dx, dy, kind, ux, uy):
        there = row_id(dx - ux, dy - uy, kind)
        return pltpu.make_async_remote_copy(
            src_ref=rim.at[m, row_id(dx, dy, kind)],
            dst_ref=rim.at[m, there],
            send_sem=send_sem.at[m, there],
            recv_sem=recv_sem.at[m, there],
            device_id=beside(ux, uy),
            device_id_type=MESH,
        )

    flying = {}

    def send(m, dx, dy, kind, ux, uy):
        copy = row_copy(m, dx, dy, kind, ux, uy)
        copy.start()
        flying[m, dx - ux, dy - uy, kind] = copy

    def initial(m):
        send(m, 0, 1, C, 0, 1)
        send(m, 0, -1, D, 0, -1)
        send(m, 1, 0, A, 1, 0)
        send(m, -1, 0, B, -1, 0)
        for u in (1, -1):
            send(m, 1, 0, A, 0, u)
            send(m, -1, 0, B, 0, u)
        for u in (1, -1):
            send(m, 0, 1, C, u, 0)
            send(m, 0, -1, D, u, 0)

    near_copies = []

    def tell_pattern():
        for k, (ux, uy) in enumerate(AROUND):
            there = row_id(-ux, -uy, 0) // TYPES
            copy = pltpu.make_async_remote_copy(
                src_ref=near.at[4],
                dst_ref=near.at[there],
                send_sem=near_send.at[there],
                recv_sem=near_recv.at[there],
                device_id=beside(ux, uy),
                device_id_type=MESH,
            )
            copy.start()
            near_copies.append(copy)

    tell_pattern()
    initial(OVL)
    initial(DEN)

    def arrive(m, dx, dy, kind):
        flying[m, dx, dy, kind].wait_recv()

    def first_tier(m):
        arrive(m, 0, 0, C)
        send(m, 0, 0, C, 0, 1)
        for u in (1, -1):
            send(m, 0, 0, C, u, 0)
        arrive(m, 0, 0, D)
        send(m, 0, 0, D, 0, -1)
        for u in (1, -1):
            send(m, 0, 0, D, u, 0)
        arrive(m, 0, 0, A)
        send(m, 0, 0, A, 1, 0)
        arrive(m, 0, 0, B)
        send(m, 0, 0, B, -1, 0)
        for u in (1, -1):
            arrive(m, 1, u, A)
            send(m, 1, u, A, 1, 0)
            arrive(m, -1, u, B)
            send(m, -1, u, B, -1, 0)

    def second_tier(m):
        arrive(m, 0, -1, C)
        for u in (1, -1):
            send(m, 0, -1, C, u, 0)
        arrive(m, 0, 1, D)
        for u in (1, -1):
            send(m, 0, 1, D, u, 0)
        for u in (1, -1):
            arrive(m, 0, u, A)
            send(m, 0, u, A, 1, 0)
            arrive(m, 0, u, B)
            send(m, 0, u, B, -1, 0)

    half = lax.broadcasted_iota(I32, (16, 128), 1) < SIDE

    def split_row(m, which, tiles, scale=None):
        def strip(k, carry):
            rows = pl.ds(pl.multiple_of(k * 16, 16), 16)
            for pair in range(KEPT // 2):
                v = rim[m, which, rows, pair * 128 : (pair + 1) * 128]
                if scale is not None:
                    v = v * scale
                top = v.astype(BF16).astype(F32)
                rest = pltpu.roll(v - top, SIDE, 1)
                tiles[(which + 1) * KEPT + 2 * pair, rows, :] = jnp.where(half, top, rest).astype(BF16)
                tiles[(which + 1) * KEPT + 2 * pair + 1, rows, :] = jnp.where(half, rest, top).astype(BF16)
            return carry

        lax.fori_loop(0, SIDE // 16, strip, 0)

    def split_left(into, i, columns, v):
        top = v.astype(BF16)
        lhs[into, i, 0:SIDE, columns] = top
        lhs[into, i, SIDE : 2 * SIDE, columns] = (v - top.astype(F32)).astype(BF16)

    def left_rows(m, scale=None):
        for i in range(TYPES):
            v = rim[m, row_id(0, 0, i)]
            split_left(0, i, slice(None), v if scale is None else v * scale)

    wide = lax.broadcasted_iota(I32, (SIDE, 128), 1) < SIDE

    def product(left, tiles, emit, after=None, carry=0):
        def one_row(i, carry):
            a = lhs[left, i]
            for pair in range(KEPT // 2):
                right = jnp.concatenate(
                    [
                        jnp.concatenate([tiles[index_s[i * KEPT + b, e]] for e in range(KEPT)], axis=0)
                        for b in (2 * pair, 2 * pair + 1)
                    ],
                    axis=1,
                )
                full = jnp.dot(a, right, preferred_element_type=F32)
                both = full[:SIDE] + full[SIDE:]
                even, odd = both[:, :128], both[:, 128:]
                even = even + pltpu.roll(even, SIDE, 1)
                odd = odd + pltpu.roll(odd, SIDE, 1)
                carry = emit(i, slice(pair * 128, (pair + 1) * 128), jnp.where(wide, even, odd), carry)
            if after is not None:
                after(i)
            return carry

        return lax.fori_loop(0, TYPES, one_row, carry)

    def to_left(into):
        def emit(i, columns, v, carry):
            split_left(into, i, columns, v)
            return carry

        return emit

    def to_left_and_second(into):
        def emit(i, columns, v, carry):
            split_left(into, i, columns, v)
            second[i, :, columns] = v
            return carry

        return emit

    own = row_id(0, 0, 0)

    for k in range(KEPT):
        tiles_s[k] = jnp.zeros((SIDE, 128), BF16)
        tiles_p[k] = jnp.zeros((SIDE, 128), BF16)
    for copy in near_copies:
        copy.wait_recv()
    to_scalars = pltpu.make_async_copy(near, near_s, local_sem.at[0])
    to_scalars.start()
    to_scalars.wait()

    first_tier(OVL)

    for kind in range(TYPES):
        slot = leaving[BEHIND[kind]]
        mine = jnp.zeros((8, 128), I32)
        for b in range(KEPT):
            mine = jnp.where(sub == b, domain_key(codes[slot, b]) + slots[slot, b], mine)
        found = jnp.zeros((8, 128), I32)
        for a in range(KEPT):
            code = codes[slot, a]
            what = near_s[code, TYPES, slots[slot, a]]
            keys = near[code, pl.ds(what, 1), :] + domain_key(code)
            hit = (keys == mine) & (lane < KEPT)
            tile = jnp.where(hit, (code * TYPES + what + 1) * KEPT + lane, 0)
            found = jnp.where(lane == a, jnp.sum(tile, axis=1, keepdims=True), found)
        index_v[kind * KEPT : (kind + 1) * KEPT, :] = found
    to_scalars = pltpu.make_async_copy(index_v, index_s, local_sem.at[1])
    to_scalars.start()
    to_scalars.wait()

    second_tier(OVL)
    first_tier(DEN)
    left_rows(DEN)

    def middle(m, tiles, scale=None):
        for dy in (0, 1, -1):
            for kind in range(TYPES):
                split_row(m, row_id(0, dy, kind), tiles, scale)
        for dy in (0, 1, -1):
            split_row(m, row_id(1, dy, A), tiles, scale)
            split_row(m, row_id(-1, dy, B), tiles, scale)

    def third_tier(m, tiles):
        for dy in (0, 1, -1):
            for u, kinds in ((1, (B, C, D)), (-1, (A, C, D))):
                for kind in kinds:
                    arrive(m, u, dy, kind)
                    split_row(m, row_id(u, dy, kind), tiles)

    middle(OVL, tiles_s)
    third_tier(OVL, tiles_s)
    second_tier(DEN)

    ham_copies = []
    for kind in range(TYPES):
        ham_out[kind] = ham[0, 0, leaving[kind]]
    for kind, (ux, uy) in enumerate(((1, 0), (-1, 0), (0, 1), (0, -1))):
        copy = pltpu.make_async_remote_copy(
            src_ref=ham_out.at[kind],
            dst_ref=ham_home.at[kind],
            send_sem=ham_send.at[kind],
            recv_sem=ham_recv.at[kind],
            device_id=beside(ux, uy),
            device_id_type=MESH,
        )
        copy.start()
        ham_copies.append(copy)

    product(0, tiles_s, to_left(1))
    middle(DEN, tiles_p)
    third_tier(DEN, tiles_p)
    product(1, tiles_p, to_left_and_second(0))
    product(0, tiles_s, to_left(1))

    def mixed_out(i, columns, v, total):
        m = 3.0 * second[i, :, columns] - 2.0 * v
        rim[MIX, own + i, :, columns] = m
        return total + folded(m * rim[OVL, own + i, :, columns])

    def mixed_sent(i):
        for ux, uy in ((0, 1), (0, -1), (1, 0), (-1, 0)):
            row_copy(MIX, 0, 0, i, ux, uy).start()

    count = product(1, tiles_p, mixed_out, mixed_sent, jnp.zeros((8, 128), F32))

    def near_copy(s, j, mine):
        return pltpu.make_async_remote_copy(
            src_ref=near_sums.at[s, at_low],
            dst_ref=near_sums.at[s, mine],
            send_sem=sum_send.at[s, 0, j],
            recv_sem=sum_recv.at[s, 0, mine],
            device_id=near_peer(j),
            device_id_type=MESH,
        )

    def far_copy(s, j, mine):
        return pltpu.make_async_remote_copy(
            src_ref=far_sums.at[s, at_high],
            dst_ref=far_sums.at[s, mine],
            send_sem=sum_send.at[s, 1, j],
            recv_sem=sum_recv.at[s, 1, mine],
            device_id=far_peer(j),
            device_id_type=MESH,
        )

    def spread(copy_of, s, me, members):
        def step(o, carry):
            copy_of(s, (me + o) % members, me).start()
            return carry

        lax.fori_loop(1, members, step, 0)

    def collect(copy_of, s, me, members):
        def step(o, carry):
            j = (me + o) % members
            copy_of(s, j, j).wait_recv()
            return carry

        lax.fori_loop(1, members, step, 0)

    def sent(copy_of, s, me, members):
        def step(o, carry):
            copy_of(s, (me + o) % members, me).wait_send()
            return carry

        lax.fori_loop(1, members, step, 0)

    near_sums[0, at_low, 0] = start
    near_sums[0, at_low, 1] = count
    near_sums[0, at_low, 2] = count
    spread(near_copy, 0, at_low, group)


    def pass_on(i):
        for dy in (-1, 1):
            row_copy(MIX, 0, 0, i, 0, -dy).wait_recv()
            for u in (1, -1):
                row_copy(MIX, 0, dy, i, u, 0).start()

    pass_on(0)
    collect(near_copy, 0, at_low, group)
    far_sums[0, at_high, 0] = jnp.sum(near_sums[0, :, 0], axis=0)
    far_sums[0, at_high, 1] = jnp.sum(near_sums[0, :, 1], axis=0)
    far_sums[0, at_high, 2] = count
    spread(far_copy, 0, at_high, high)
    pass_on(1)
    pass_on(2)
    pass_on(3)
    collect(far_copy, 0, at_high, high)

    def over_all(tile):
        return jnp.sum(jnp.sum(tile, axis=1, keepdims=True), axis=0, keepdims=True)

    count_start = over_all(jnp.sum(far_sums[0, :, 0], axis=0))
    scale = count_start / over_all(jnp.sum(far_sums[0, :, 1], axis=0))
    left_rows(MIX, scale)
    product(0, tiles_s, to_left(1))
    for dy in (0, -1, 1):
        for kind in range(TYPES):
            split_row(MIX, row_id(0, dy, kind), tiles_p, scale)
    for dy in (0, -1, 1):
        for u in (1, -1):
            for kind in range(TYPES):
                row_copy(MIX, 0, dy, kind, -u, 0).wait_recv()
                split_row(MIX, row_id(u, dy, kind), tiles_p, scale)
    product(1, tiles_p, to_left_and_second(0))
    product(0, tiles_s, to_left(1))

    def last_out(i, columns, v, carry):
        total, largest = carry
        m = 3.0 * second[i, :, columns] - 2.0 * v
        last[i, :, columns] = m
        return (
            total + folded(m * rim[OVL, own + i, :, columns]),
            jnp.maximum(largest, jnp.max(jnp.abs(m).reshape(SIDE // 8, 8, 128), axis=0)),
        )

    zero = jnp.zeros((8, 128), F32)
    count, largest = product(1, tiles_p, last_out, None, (zero, zero))
    for copy in ham_copies:
        copy.wait_recv()
    largest = jnp.max(jnp.max(largest, axis=1, keepdims=True), axis=0, keepdims=True)
    size = jnp.where(largest > 1e-37, jnp.minimum(largest, 1e37), 1.0)
    inverse = 1.0 / size
    band = zero
    for i in range(TYPES):
        for k in range(COLUMNS // 128):
            columns = slice(k * 128, (k + 1) * 128)
            band += folded((last[i, :, columns] * inverse) * ham_home[i, :, columns])

    def joined(sums):
        sizes = sums[:, 2]
        biggest = jnp.max(sizes, axis=0)
        return jnp.sum(sums[:, 0], axis=0), jnp.sum(sums[:, 1] * (sizes / biggest[None]), axis=0), biggest

    near_sums[1, at_low, 0] = count
    near_sums[1, at_low, 1] = band
    near_sums[1, at_low, 2] = jnp.broadcast_to(size, (8, 128))
    spread(near_copy, 1, at_low, group)
    collect(near_copy, 1, at_low, group)
    part = joined(near_sums[1])
    for k in range(3):
        far_sums[1, at_high, k] = part[k]
    spread(far_copy, 1, at_high, high)
    collect(far_copy, 1, at_high, high)
    count, band, size = joined(far_sums[1])
    scale = count_start / over_all(count)
    for slot in range(TYPES):
        out[0, 0, slot] = scale * last[near_s[4, TYPES, slot]]
    basis = nx * ny * TYPES * SIDE
    energy[0] = jnp.sum(over_all(band * (size * scale))) / basis

    for copy in (*near_copies, *ham_copies, *flying.values()):
        copy.wait_send()
    for i in range(TYPES):
        for ux, uy in ((0, 1), (0, -1), (1, 0), (-1, 0)):
            row_copy(MIX, 0, 0, i, ux, uy).wait_send()
        for dy in (-1, 1):
            for u in (1, -1):
                row_copy(MIX, 0, dy, i, u, 0).wait_send()
    for s in range(2):
        sent(near_copy, s, at_low, group)
        sent(far_copy, s, at_high, high)


def shards(nx, ny, ham, ovl, den, leaving, codes, slots):
    high, group = nx // LOW, LOW * ny
    vmem = pl.BlockSpec(memory_space=pltpu.VMEM)
    smem = pl.BlockSpec(memory_space=pltpu.SMEM)
    dma = pltpu.SemaphoreType.DMA
    purified, energy = pl.pallas_call(
        functools.partial(kernel, nx, ny),
        out_shape=(
            jax.ShapeDtypeStruct(den.shape, F32),
            jax.ShapeDtypeStruct((1,), F32),
        ),
        in_specs=[vmem] * 3 + [smem] * 3,
        out_specs=(vmem, smem),
        scratch_shapes=[
            pltpu.VMEM((3, 9 * TYPES, SIDE, COLUMNS), F32),
            pltpu.VMEM((TYPES, SIDE, COLUMNS), F32),
            pltpu.VMEM((TYPES, SIDE, COLUMNS), F32),
            pltpu.VMEM(((9 * TYPES + 1) * KEPT, SIDE, 128), BF16),
            pltpu.VMEM(((9 * TYPES + 1) * KEPT, SIDE, 128), BF16),
            pltpu.VMEM((2, TYPES, 2 * SIDE, COLUMNS), BF16),
            pltpu.VMEM((TYPES, SIDE, COLUMNS), F32),
            pltpu.VMEM((TYPES, SIDE, COLUMNS), F32),
            pltpu.VMEM((9, 8, 128), I32),
            pltpu.SMEM((9, 8, 128), I32),
            pltpu.VMEM((TYPES * KEPT, 128), I32),
            pltpu.SMEM((TYPES * KEPT, 128), I32),
            pltpu.VMEM((2, group, 3, 8, 128), F32),
            pltpu.VMEM((2, high, 3, 8, 128), F32),
            dma((3, 9 * TYPES)),
            dma((3, 9 * TYPES)),
            dma((TYPES,)),
            dma((TYPES,)),
            dma((9,)),
            dma((9,)),
            dma((2, 2, max(group, high))),
            dma((2, 2, max(group, high))),
            dma((2,)),
        ],
        compiler_params=pltpu.CompilerParams(
            collective_id=0, has_side_effects=True, vmem_limit_bytes=48 * 1024 * 1024
        ),
    )(
        ham, ovl, den,
        leaving.reshape(TYPES), codes.reshape(TYPES, KEPT), slots.reshape(TYPES, KEPT),
    )
    return purified, energy.reshape(())


def solution(mesh):
    whole = P("gx", "gy", None, None, None)
    few = P("gx", "gy", None, None)
    return jax.shard_map(
        functools.partial(shards, mesh.shape["gx"], mesh.shape["gy"]),
        mesh=mesh,
        in_specs=(whole, whole, whole, few, few, few),
        out_specs=(whole, P()),
        check_vma=False,
    )
```

```python
import functools

import jax
import jax.numpy as jnp
from jax import lax
from jax.experimental import pallas as pl
from jax.experimental.pallas import tpu as pltpu
from jax.sharding import PartitionSpec as P

MESH = pl.DeviceIdType.MESH
F32, BF16, I32 = jnp.float32, jnp.bfloat16, jnp.int32
A, B, C, D = range(4)
SIDE, KEPT, TYPES = 64, 8, 4
COLUMNS = SIDE * KEPT
OVL, DEN, MIX = range(3)
BEHIND = (1, 0, 3, 2)
AROUND = [(ux, uy) for ux in (-1, 0, 1) for uy in (-1, 0, 1) if (ux, uy) != (0, 0)]
LOW = 4


def row_id(dx, dy, kind):
    return (3 * (dx + 1) + (dy + 1)) * TYPES + kind


def domain_key(code):
    across = (code * 11) >> 5
    return (across - 1) * 64 + (code - 3 * across - 1) * 8


def folded(tile):
    return jnp.sum(tile.reshape(tile.shape[0] // 8, 8, 128), axis=0)


def kernel(
    nx, ny,
    ham, ovl, den, leaving, codes, slots,
    out, energy,
    rim, ham_out, ham_home, tiles_s, tiles_p, lhs, second, last,
    near, near_s, index_v, index_s, near_sums, far_sums,
    send_sem, recv_sem, ham_send, ham_recv, near_send, near_recv, sum_send, sum_recv, local_sem,
):
    x, y = lax.axis_index("gx"), lax.axis_index("gy")
    high = nx // LOW
    group = LOW * ny
    at_high, at_low = x // LOW, (x % LOW) * ny + y

    def beside(ux, uy):
        return (lax.rem(x + ux + nx, nx), lax.rem(y + uy + ny, ny))

    def near_peer(j):
        return (at_high * LOW + j // ny, j % ny)

    def far_peer(j):
        return (j * LOW + x % LOW, y)

    barrier = pltpu.get_barrier_semaphore()
    for ux, uy in AROUND:
        pl.semaphore_signal(barrier, inc=1, device_id=beside(ux, uy), device_id_type=MESH)

    def greet_near(o, carry):
        pl.semaphore_signal(barrier, inc=1, device_id=near_peer((at_low + o) % group), device_id_type=MESH)
        return carry

    def greet_far(o, carry):
        pl.semaphore_signal(barrier, inc=1, device_id=far_peer((at_high + o) % high), device_id_type=MESH)
        return carry

    lax.fori_loop(1, group, greet_near, 0)
    lax.fori_loop(1, high, greet_far, 0)

    lane = lax.broadcasted_iota(I32, (8, 128), 1)
    sub = lax.broadcasted_iota(I32, (8, 128), 0)

    start = jnp.zeros((8, 128), F32)
    for kind in range(TYPES):
        slot = leaving[kind]
        mine = row_id(*((1, 0), (-1, 0), (0, 1), (0, -1))[kind], kind)
        s_row, p_row = ovl[0, 0, slot], den[0, 0, slot]
        rim[OVL, mine] = s_row
        rim[DEN, mine] = p_row
        prod = s_row * p_row
        for k in range(COLUMNS // 128):
            start += folded(prod[:, k * 128 : (k + 1) * 128])

    note = jnp.zeros((8, 128), I32)
    for kind in range(TYPES):
        slot = leaving[BEHIND[kind]]
        for c in range(KEPT):
            key = domain_key(codes[slot, c]) + slots[slot, c]
            note = jnp.where((sub == kind) & (lane == c), key, note)
        note = jnp.where((sub == TYPES) & (lane == slot), kind, note)
    near[4] = note

    pl.semaphore_wait(barrier, len(AROUND) + group - 1 + high - 1)

    def row_copy(m, dx, dy, kind, ux, uy):
        there = row_id(dx - ux, dy - uy, kind)
        return pltpu.make_async_remote_copy(
            src_ref=rim.at[m, row_id(dx, dy, kind)],
            dst_ref=rim.at[m, there],
            send_sem=send_sem.at[m, there],
            recv_sem=recv_sem.at[m, there],
            device_id=beside(ux, uy),
            device_id_type=MESH,
        )

    flying = {}

    def send(m, dx, dy, kind, ux, uy):
        copy = row_copy(m, dx, dy, kind, ux, uy)
        copy.start()
        flying[m, dx - ux, dy - uy, kind] = copy

    def initial(m):
        send(m, 0, 1, C, 0, 1)
        send(m, 0, -1, D, 0, -1)
        send(m, 1, 0, A, 1, 0)
        send(m, -1, 0, B, -1, 0)
        for u in (1, -1):
            send(m, 1, 0, A, 0, u)
            send(m, -1, 0, B, 0, u)
        for u in (1, -1):
            send(m, 0, 1, C, u, 0)
            send(m, 0, -1, D, u, 0)

    near_copies = []

    def tell_pattern():
        for k, (ux, uy) in enumerate(AROUND):
            there = row_id(-ux, -uy, 0) // TYPES
            copy = pltpu.make_async_remote_copy(
                src_ref=near.at[4],
                dst_ref=near.at[there],
                send_sem=near_send.at[there],
                recv_sem=near_recv.at[there],
                device_id=beside(ux, uy),
                device_id_type=MESH,
            )
            copy.start()
            near_copies.append(copy)

    tell_pattern()
    initial(OVL)
    initial(DEN)

    def arrive(m, dx, dy, kind):
        flying[m, dx, dy, kind].wait_recv()

    def first_tier(m):
        arrive(m, 0, 0, C)
        send(m, 0, 0, C, 0, 1)
        for u in (1, -1):
            send(m, 0, 0, C, u, 0)
        arrive(m, 0, 0, D)
        send(m, 0, 0, D, 0, -1)
        for u in (1, -1):
            send(m, 0, 0, D, u, 0)
        arrive(m, 0, 0, A)
        send(m, 0, 0, A, 1, 0)
        arrive(m, 0, 0, B)
        send(m, 0, 0, B, -1, 0)
        for u in (1, -1):
            arrive(m, 1, u, A)
            send(m, 1, u, A, 1, 0)
            arrive(m, -1, u, B)
            send(m, -1, u, B, -1, 0)

    def second_tier(m):
        arrive(m, 0, -1, C)
        for u in (1, -1):
            send(m, 0, -1, C, u, 0)
        arrive(m, 0, 1, D)
        for u in (1, -1):
            send(m, 0, 1, D, u, 0)
        for u in (1, -1):
            arrive(m, 0, u, A)
            send(m, 0, u, A, 1, 0)
            arrive(m, 0, u, B)
            send(m, 0, u, B, -1, 0)

    half = lax.broadcasted_iota(I32, (SIDE, 128), 1) < SIDE

    def split_row(m, which, tiles, scale=None):
        for pair in range(KEPT // 2):
            v = rim[m, which, :, pair * 128 : (pair + 1) * 128]
            if scale is not None:
                v = v * scale
            top = v.astype(BF16)
            rest = pltpu.roll((v - top.astype(F32)).astype(BF16), SIDE, 1)
            tiles[(which + 1) * KEPT + 2 * pair] = jnp.where(half, top, rest)
            tiles[(which + 1) * KEPT + 2 * pair + 1] = jnp.where(half, rest, top)

    def split_left(into, i, columns, v):
        top = v.astype(BF16)
        lhs[into, i, 0:SIDE, columns] = top
        lhs[into, i, SIDE : 2 * SIDE, columns] = (v - top.astype(F32)).astype(BF16)

    def left_rows(m, scale=None):
        for i in range(TYPES):
            v = rim[m, row_id(0, 0, i)]
            split_left(0, i, slice(None), v if scale is None else v * scale)

    wide = lax.broadcasted_iota(I32, (SIDE, 128), 1) < SIDE

    def product(left, tiles, emit, after=None, carry=0):
        def one_row(i, carry):
            a = lhs[left, i]
            for pair in range(KEPT // 2):
                right = jnp.concatenate(
                    [
                        jnp.concatenate([tiles[index_s[i * KEPT + b, e]] for e in range(KEPT)], axis=0)
                        for b in (2 * pair, 2 * pair + 1)
                    ],
                    axis=1,
                )
                full = jnp.dot(a, right, preferred_element_type=F32)
                both = full[:SIDE] + full[SIDE:]
                even, odd = both[:, :128], both[:, 128:]
                even = even + pltpu.roll(even, SIDE, 1)
                odd = odd + pltpu.roll(odd, SIDE, 1)
                carry = emit(i, slice(pair * 128, (pair + 1) * 128), jnp.where(wide, even, odd), carry)
            if after is not None:
                after(i)
            return carry

        return lax.fori_loop(0, TYPES, one_row, carry)

    def to_left(into):
        def emit(i, columns, v, carry):
            split_left(into, i, columns, v)
            return carry

        return emit

    def to_left_and_second(into):
        def emit(i, columns, v, carry):
            split_left(into, i, columns, v)
            second[i, :, columns] = v
            return carry

        return emit

    own = row_id(0, 0, 0)

    for k in range(KEPT):
        tiles_s[k] = jnp.zeros((SIDE, 128), BF16)
        tiles_p[k] = jnp.zeros((SIDE, 128), BF16)
    for copy in near_copies:
        copy.wait_recv()
    to_scalars = pltpu.make_async_copy(near, near_s, local_sem.at[0])
    to_scalars.start()
    to_scalars.wait()

    first_tier(OVL)

    for kind in range(TYPES):
        slot = leaving[BEHIND[kind]]
        mine = jnp.zeros((8, 128), I32)
        for b in range(KEPT):
            mine = jnp.where(sub == b, domain_key(codes[slot, b]) + slots[slot, b], mine)
        found = jnp.zeros((8, 128), I32)
        for a in range(KEPT):
            code = codes[slot, a]
            what = near_s[code, TYPES, slots[slot, a]]
            keys = near[code, pl.ds(what, 1), :] + domain_key(code)
            hit = (keys == mine) & (lane < KEPT)
            tile = jnp.where(hit, (code * TYPES + what + 1) * KEPT + lane, 0)
            found = jnp.where(lane == a, jnp.sum(tile, axis=1, keepdims=True), found)
        index_v[kind * KEPT : (kind + 1) * KEPT, :] = found
    to_scalars = pltpu.make_async_copy(index_v, index_s, local_sem.at[1])
    to_scalars.start()
    to_scalars.wait()

    second_tier(OVL)
    first_tier(DEN)
    left_rows(DEN)

    def landed(m, which):
        pltpu.make_async_remote_copy(
            src_ref=rim.at[m, which],
            dst_ref=rim.at[m, which],
            send_sem=send_sem.at[m, which],
            recv_sem=recv_sem.at[m, which],
            device_id=beside(1, 0),
            device_id_type=MESH,
        ).wait_recv()

    def middle(m, tiles):
        def one(j, carry):
            split_row(m, row_id(0, -1, 0) + j, tiles)
            return carry

        def sides(j, carry):
            split_row(m, row_id(1, -1, A) + j * TYPES, tiles)
            split_row(m, row_id(-1, -1, B) + j * TYPES, tiles)
            return carry

        lax.fori_loop(0, 3 * TYPES, one, 0)
        lax.fori_loop(0, 3, sides, 0)

    def third_tier(m, tiles):
        def one(j, carry):
            skip = lax.rem(j + 1, 3) * TYPES
            for u, kinds in ((1, (B, C, D)), (-1, (A, C, D))):
                for kind in kinds:
                    which = row_id(u, -1, kind) + skip
                    landed(m, which)
                    split_row(m, which, tiles)
            return carry

        lax.fori_loop(0, 3, one, 0)

    middle(OVL, tiles_s)
    third_tier(OVL, tiles_s)
    second_tier(DEN)

    ham_copies = []
    for kind in range(TYPES):
        ham_out[kind] = ham[0, 0, leaving[kind]]
    for kind, (ux, uy) in enumerate(((1, 0), (-1, 0), (0, 1), (0, -1))):
        copy = pltpu.make_async_remote_copy(
            src_ref=ham_out.at[kind],
            dst_ref=ham_home.at[kind],
            send_sem=ham_send.at[kind],
            recv_sem=ham_recv.at[kind],
            device_id=beside(ux, uy),
            device_id_type=MESH,
        )
        copy.start()
        ham_copies.append(copy)

    product(0, tiles_s, to_left(1))
    middle(DEN, tiles_p)
    third_tier(DEN, tiles_p)
    product(1, tiles_p, to_left_and_second(0))
    product(0, tiles_s, to_left(1))

    def mixed_out(i, columns, v, total):
        m = 3.0 * second[i, :, columns] - 2.0 * v
        rim[MIX, own + i, :, columns] = m
        return total + folded(m * rim[OVL, own + i, :, columns])

    def mixed_sent(i):
        for ux, uy in ((0, 1), (0, -1), (1, 0), (-1, 0)):
            row_copy(MIX, 0, 0, i, ux, uy).start()

    count = product(1, tiles_p, mixed_out, mixed_sent, jnp.zeros((8, 128), F32))

    def near_copy(s, j, mine):
        return pltpu.make_async_remote_copy(
            src_ref=near_sums.at[s, at_low],
            dst_ref=near_sums.at[s, mine],
            send_sem=sum_send.at[s, 0, j],
            recv_sem=sum_recv.at[s, 0, mine],
            device_id=near_peer(j),
            device_id_type=MESH,
        )

    def far_copy(s, j, mine):
        return pltpu.make_async_remote_copy(
            src_ref=far_sums.at[s, at_high],
            dst_ref=far_sums.at[s, mine],
            send_sem=sum_send.at[s, 1, j],
            recv_sem=sum_recv.at[s, 1, mine],
            device_id=far_peer(j),
            device_id_type=MESH,
        )

    def spread(copy_of, s, me, members):
        def step(o, carry):
            copy_of(s, (me + o) % members, me).start()
            return carry

        lax.fori_loop(1, members, step, 0)

    def collect(copy_of, s, me, members):
        def step(o, carry):
            j = (me + o) % members
            copy_of(s, j, j).wait_recv()
            return carry

        lax.fori_loop(1, members, step, 0)

    def sent(copy_of, s, me, members):
        def step(o, carry):
            copy_of(s, (me + o) % members, me).wait_send()
            return carry

        lax.fori_loop(1, members, step, 0)

    across = lax.broadcasted_iota(I32, (1, 128), 1)

    def over_all(tile):
        return jnp.sum(jnp.sum(tile, axis=0, keepdims=True), axis=1, keepdims=True)

    near_sums[0, at_low] = jnp.where(across < SIDE, over_all(start), over_all(count))
    spread(near_copy, 0, at_low, group)


    def pass_on(i):
        for dy in (-1, 1):
            row_copy(MIX, 0, 0, i, 0, -dy).wait_recv()
            for u in (1, -1):
                row_copy(MIX, 0, dy, i, u, 0).start()

    pass_on(0)
    collect(near_copy, 0, at_low, group)
    far_sums[0, at_high] = jnp.sum(near_sums[0], axis=0)
    spread(far_copy, 0, at_high, high)
    pass_on(1)
    pass_on(2)
    pass_on(3)
    collect(far_copy, 0, at_high, high)

    counts = jnp.sum(far_sums[0], axis=0)
    count_start = counts[:, :1]
    scale = count_start / counts[:, SIDE : SIDE + 1]
    left_rows(MIX, scale)
    product(0, tiles_s, to_left(1))

    def mixed_middle(j, carry):
        split_row(MIX, row_id(0, -1, 0) + j, tiles_p, scale)
        return carry

    def mixed_sides(j, carry):
        skip = lax.rem(j + 1, 3) * TYPES
        for kind in range(TYPES):
            for u in (1, -1):
                which = row_id(u, -1, kind) + skip
                landed(MIX, which)
                split_row(MIX, which, tiles_p, scale)
        return carry

    lax.fori_loop(0, 3 * TYPES, mixed_middle, 0)
    lax.fori_loop(0, 3, mixed_sides, 0)
    product(1, tiles_p, to_left_and_second(0))
    product(0, tiles_s, to_left(1))

    def last_out(i, columns, v, carry):
        total, largest = carry
        m = 3.0 * second[i, :, columns] - 2.0 * v
        last[i, :, columns] = m
        return (
            total + folded(m * rim[OVL, own + i, :, columns]),
            jnp.maximum(largest, jnp.max(jnp.abs(m).reshape(SIDE // 8, 8, 128), axis=0)),
        )

    zero = jnp.zeros((8, 128), F32)
    count, largest = product(1, tiles_p, last_out, None, (zero, zero))
    for copy in ham_copies:
        copy.wait_recv()
    largest = jnp.max(jnp.max(largest, axis=1, keepdims=True), axis=0, keepdims=True)
    size = jnp.where(largest > 1e-37, jnp.minimum(largest, 1e37), 1.0)
    inverse = 1.0 / size
    band = zero
    for i in range(TYPES):
        for k in range(COLUMNS // 128):
            columns = slice(k * 128, (k + 1) * 128)
            band += folded((last[i, :, columns] * inverse) * ham_home[i, :, columns])

    def joined(sums):
        biggest = jnp.max(sums, axis=0)
        ratio = pltpu.roll(sums, SIDE, 2) / pltpu.roll(biggest, SIDE, 1)[None]
        added = jnp.sum(jnp.where((across >= 32)[None], sums * ratio, sums), axis=0)
        return jnp.where(across < SIDE, added, biggest)

    near_sums[1, at_low] = jnp.where(
        across < 32, over_all(count), jnp.where(across < SIDE, over_all(band), size)
    )
    spread(near_copy, 1, at_low, group)
    collect(near_copy, 1, at_low, group)
    far_sums[1, at_high] = joined(near_sums[1])
    spread(far_copy, 1, at_high, high)
    collect(far_copy, 1, at_high, high)
    sums = joined(far_sums[1])
    scale = count_start / sums[:, :1]
    for slot in range(TYPES):
        out[0, 0, slot] = scale * last[near_s[4, TYPES, slot]]
    basis = nx * ny * TYPES * SIDE
    energy[0] = jnp.sum(sums[:, 32:33] * (sums[:, SIDE : SIDE + 1] * scale)) / basis

    for copy in (*near_copies, *ham_copies, *flying.values()):
        copy.wait_send()
    for i in range(TYPES):
        for ux, uy in ((0, 1), (0, -1), (1, 0), (-1, 0)):
            row_copy(MIX, 0, 0, i, ux, uy).wait_send()
        for dy in (-1, 1):
            for u in (1, -1):
                row_copy(MIX, 0, dy, i, u, 0).wait_send()
    for s in range(2):
        sent(near_copy, s, at_low, group)
        sent(far_copy, s, at_high, high)


def shards(nx, ny, ham, ovl, den, leaving, codes, slots):
    high, group = nx // LOW, LOW * ny
    vmem = pl.BlockSpec(memory_space=pltpu.VMEM)
    smem = pl.BlockSpec(memory_space=pltpu.SMEM)
    dma = pltpu.SemaphoreType.DMA
    purified, energy = pl.pallas_call(
        functools.partial(kernel, nx, ny),
        out_shape=(
            jax.ShapeDtypeStruct(den.shape, F32),
            jax.ShapeDtypeStruct((1,), F32),
        ),
        in_specs=[vmem] * 3 + [smem] * 3,
        out_specs=(vmem, smem),
        scratch_shapes=[
            pltpu.VMEM((3, 9 * TYPES, SIDE, COLUMNS), F32),
            pltpu.VMEM((TYPES, SIDE, COLUMNS), F32),
            pltpu.VMEM((TYPES, SIDE, COLUMNS), F32),
            pltpu.VMEM(((9 * TYPES + 1) * KEPT, SIDE, 128), BF16),
            pltpu.VMEM(((9 * TYPES + 1) * KEPT, SIDE, 128), BF16),
            pltpu.VMEM((2, TYPES, 2 * SIDE, COLUMNS), BF16),
            pltpu.VMEM((TYPES, SIDE, COLUMNS), F32),
            pltpu.VMEM((TYPES, SIDE, COLUMNS), F32),
            pltpu.VMEM((9, 8, 128), I32),
            pltpu.SMEM((9, 8, 128), I32),
            pltpu.VMEM((TYPES * KEPT, 128), I32),
            pltpu.SMEM((TYPES * KEPT, 128), I32),
            pltpu.VMEM((2, group, 1, 128), F32),
            pltpu.VMEM((2, high, 1, 128), F32),
            dma((3, 9 * TYPES)),
            dma((3, 9 * TYPES)),
            dma((TYPES,)),
            dma((TYPES,)),
            dma((9,)),
            dma((9,)),
            dma((2, 2, max(group, high))),
            dma((2, 2, max(group, high))),
            dma((2,)),
        ],
        compiler_params=pltpu.CompilerParams(
            collective_id=0, has_side_effects=True, vmem_limit_bytes=48 * 1024 * 1024
        ),
    )(
        ham, ovl, den,
        leaving.reshape(TYPES), codes.reshape(TYPES, KEPT), slots.reshape(TYPES, KEPT),
    )
    return purified, energy.reshape(())


def solution(mesh):
    whole = P("gx", "gy", None, None, None)
    few = P("gx", "gy", None, None)
    return jax.shard_map(
        functools.partial(shards, mesh.shape["gx"], mesh.shape["gy"]),
        mesh=mesh,
        in_specs=(whole, whole, whole, few, few, few),
        out_specs=(whole, P()),
        check_vma=False,
    )
```

```python
import functools

import jax
import jax.numpy as jnp
from jax import lax
from jax.experimental import pallas as pl
from jax.experimental.pallas import tpu as pltpu
from jax.sharding import PartitionSpec as P

MESH = pl.DeviceIdType.MESH
F32, BF16, I32 = jnp.float32, jnp.bfloat16, jnp.int32
A, B, C, D = range(4)
SIDE, KEPT, TYPES = 64, 8, 4
COLUMNS = SIDE * KEPT
OVL, DEN, MIX = range(3)
BEHIND = (1, 0, 3, 2)
AROUND = [(ux, uy) for ux in (-1, 0, 1) for uy in (-1, 0, 1) if (ux, uy) != (0, 0)]
LOW = 4


def row_id(dx, dy, kind):
    return (3 * (dx + 1) + (dy + 1)) * TYPES + kind


def domain_key(code):
    across = (code * 11) >> 5
    return (across - 1) * 64 + (code - 3 * across - 1) * 8


def folded(tile):
    return jnp.sum(tile.reshape(tile.shape[0] // 8, 8, 128), axis=0)


def kernel(
    nx, ny,
    ham_hbm, ovl_hbm, den_hbm, leaving_hbm, codes_hbm, slots_hbm,
    out, energy,
    ham, ovl, den, leaving, codes, slots,
    rim, ham_out, ham_home, tiles_s, tiles_p, lhs, second, last,
    near, near_s, index_v, index_s, near_sums, far_sums,
    send_sem, recv_sem, ham_send, ham_recv, near_send, near_recv, sum_send, sum_recv, local_sem, load_sem,
):
    x, y = lax.axis_index("gx"), lax.axis_index("gy")
    high = nx // LOW
    group = LOW * ny
    at_high, at_low = x // LOW, (x % LOW) * ny + y

    def beside(ux, uy):
        return (lax.rem(x + ux + nx, nx), lax.rem(y + uy + ny, ny))

    def near_peer(j):
        return (at_high * LOW + j // ny, j % ny)

    def far_peer(j):
        return (j * LOW + x % LOW, y)

    loads = [
        pltpu.make_async_copy(there, here, load_sem.at[k])
        for k, (there, here) in enumerate((
            (leaving_hbm, leaving), (codes_hbm, codes), (slots_hbm, slots),
            (ovl_hbm, ovl), (den_hbm, den), (ham_hbm, ham),
        ))
    ]
    for load in loads:
        load.start()

    barrier = pltpu.get_barrier_semaphore()
    for ux, uy in AROUND:
        pl.semaphore_signal(barrier, inc=1, device_id=beside(ux, uy), device_id_type=MESH)

    def greet_near(o, carry):
        pl.semaphore_signal(barrier, inc=1, device_id=near_peer((at_low + o) % group), device_id_type=MESH)
        return carry

    def greet_far(o, carry):
        pl.semaphore_signal(barrier, inc=1, device_id=far_peer((at_high + o) % high), device_id_type=MESH)
        return carry

    lax.fori_loop(1, group, greet_near, 0)
    lax.fori_loop(1, high, greet_far, 0)

    lane = lax.broadcasted_iota(I32, (8, 128), 1)
    sub = lax.broadcasted_iota(I32, (8, 128), 0)

    for load in loads[:3]:
        load.wait()
    note = jnp.zeros((8, 128), I32)
    for kind in range(TYPES):
        slot = leaving[BEHIND[kind]]
        for c in range(KEPT):
            key = domain_key(codes[slot, c]) + slots[slot, c]
            note = jnp.where((sub == kind) & (lane == c), key, note)
        note = jnp.where((sub == TYPES) & (lane == slot), kind, note)
    near[4] = note

    for load in loads[3:5]:
        load.wait()
    start = jnp.zeros((8, 128), F32)
    for kind in range(TYPES):
        slot = leaving[kind]
        mine = row_id(*((1, 0), (-1, 0), (0, 1), (0, -1))[kind], kind)
        s_row, p_row = ovl[slot], den[slot]
        rim[OVL, mine] = s_row
        rim[DEN, mine] = p_row
        prod = s_row * p_row
        for k in range(COLUMNS // 128):
            start += folded(prod[:, k * 128 : (k + 1) * 128])

    pl.semaphore_wait(barrier, len(AROUND) + group - 1 + high - 1)

    def row_copy(m, which, there, ux, uy, left=None):
        return pltpu.make_async_remote_copy(
            src_ref=rim.at[m, which],
            dst_ref=rim.at[m, there],
            send_sem=send_sem.at[m, there if left is None else left],
            recv_sem=recv_sem.at[m, there],
            device_id=beside(ux, uy),
            device_id_type=MESH,
        )

    def send(m, dx, dy, kind, ux, uy):
        row_copy(m, row_id(dx, dy, kind), row_id(dx - ux, dy - uy, kind), ux, uy).start()

    def landed(m, which):
        row_copy(m, which, which, 1, 0).wait_recv()

    def arrive(m, dx, dy, kind):
        landed(m, row_id(dx, dy, kind))

    core = lax.rem(x, 2)
    outer, inner = 2 * core - 1, 1 - 2 * core
    outer_ids, inner_ids = core * (6 * TYPES), (1 - core) * (6 * TYPES)

    def outer_id(dy, kind):
        return outer_ids + ((dy + 1) * TYPES + kind)

    def send_inner(m, dy, kind):
        left = inner_ids + ((dy + 1) * TYPES + kind)
        row_copy(m, row_id(0, dy, kind), outer_id(dy, kind), inner, 0, left).start()

    def outer_on(m, dy, kind, uy):
        landed(m, outer_id(dy, kind))
        row_copy(m, outer_id(dy, kind), outer_id(dy - uy, kind), 0, uy).start()

    def start_y(m):
        send(m, 0, 1, C, 0, 1)
        send(m, 0, -1, D, 0, -1)
        for u in (1, -1):
            send(m, 1, 0, A, 0, u)
            send(m, -1, 0, B, 0, u)

    def start_x(m):
        send(m, 1, 0, A, 1, 0)
        send(m, -1, 0, B, -1, 0)
        for u in (1, -1):
            send(m, 0, 1, C, u, 0)
            send(m, 0, -1, D, u, 0)

    near_copies = []

    def tell_pattern():
        for k, (ux, uy) in enumerate(AROUND):
            there = row_id(-ux, -uy, 0) // TYPES
            copy = pltpu.make_async_remote_copy(
                src_ref=near.at[4],
                dst_ref=near.at[there],
                send_sem=near_send.at[there],
                recv_sem=near_recv.at[there],
                device_id=beside(ux, uy),
                device_id_type=MESH,
            )
            copy.start()
            near_copies.append(copy)

    tell_pattern()
    start_y(OVL)
    start_x(OVL)
    start_x(DEN)

    def first_tier(m):
        for kind, uy in ((C, 1), (D, -1)):
            arrive(m, 0, 0, kind)
            send(m, 0, 0, kind, 0, uy)
            if m == OVL:
                for u in (1, -1):
                    send(m, 0, 0, kind, u, 0)
            else:
                send_inner(m, 0, kind)
        arrive(m, 0, 0, A)
        send(m, 0, 0, A, 1, 0)
        arrive(m, 0, 0, B)
        send(m, 0, 0, B, -1, 0)
        for u in (1, -1):
            arrive(m, 1, u, A)
            send(m, 1, u, A, 1, 0)
            arrive(m, -1, u, B)
            send(m, -1, u, B, -1, 0)
        if m == DEN:
            outer_on(m, 0, C, 1)
            outer_on(m, 0, D, -1)

    def second_tier(m):
        for kind, uy in ((C, 1), (D, -1)):
            arrive(m, 0, -uy, kind)
            if m == OVL:
                for u in (1, -1):
                    send(m, 0, -uy, kind, u, 0)
            else:
                send_inner(m, -uy, kind)
        for u in (1, -1):
            arrive(m, 0, u, A)
            send(m, 0, u, A, 1, 0)
            arrive(m, 0, u, B)
            send(m, 0, u, B, -1, 0)

    half = lax.broadcasted_iota(I32, (SIDE, 128), 1) < SIDE

    def split_row(m, which, tiles, scale=None):
        for pair in range(KEPT // 2):
            v = rim[m, which, :, pair * 128 : (pair + 1) * 128]
            if scale is not None:
                v = v * scale
            top = v.astype(BF16)
            rest = pltpu.roll((v - top.astype(F32)).astype(BF16), SIDE, 1)
            tiles[(which + 1) * KEPT + 2 * pair] = jnp.where(half, top, rest)
            tiles[(which + 1) * KEPT + 2 * pair + 1] = jnp.where(half, rest, top)

    def split_left(into, i, columns, v):
        top = v.astype(BF16)
        lhs[into, i, 0:SIDE, columns] = top
        lhs[into, i, SIDE : 2 * SIDE, columns] = (v - top.astype(F32)).astype(BF16)

    def left_rows(m, scale=None):
        for i in range(TYPES):
            v = rim[m, row_id(0, 0, i)]
            split_left(0, i, slice(None), v if scale is None else v * scale)

    wide = lax.broadcasted_iota(I32, (SIDE, 128), 1) < SIDE

    def product(left, tiles, emit, after=None, carry=0):
        def one_row(i, carry):
            a = lhs[left, i]
            for pair in range(KEPT // 2):
                right = jnp.concatenate(
                    [
                        jnp.concatenate([tiles[index_s[i * KEPT + b, e]] for e in range(KEPT)], axis=0)
                        for b in (2 * pair, 2 * pair + 1)
                    ],
                    axis=1,
                )
                full = jnp.dot(a, right, preferred_element_type=F32)
                both = full[:SIDE] + full[SIDE:]
                even, odd = both[:, :128], both[:, 128:]
                even = even + pltpu.roll(even, SIDE, 1)
                odd = odd + pltpu.roll(odd, SIDE, 1)
                carry = emit(i, slice(pair * 128, (pair + 1) * 128), jnp.where(wide, even, odd), carry)
            if after is not None:
                after(i)
            return carry

        return lax.fori_loop(0, TYPES, one_row, carry)

    def to_left(into):
        def emit(i, columns, v, carry):
            split_left(into, i, columns, v)
            return carry

        return emit

    def to_left_and_second(into):
        def emit(i, columns, v, carry):
            split_left(into, i, columns, v)
            second[i, :, columns] = v
            return carry

        return emit

    own = row_id(0, 0, 0)

    for k in range(KEPT):
        tiles_s[k] = jnp.zeros((SIDE, 128), BF16)
        tiles_p[k] = jnp.zeros((SIDE, 128), BF16)
    for copy in near_copies:
        copy.wait_recv()
    to_scalars = pltpu.make_async_copy(near, near_s, local_sem.at[0])
    to_scalars.start()
    to_scalars.wait()

    first_tier(OVL)
    start_y(DEN)
    outer_on(DEN, 1, C, 1)
    outer_on(DEN, -1, D, -1)

    for kind in range(TYPES):
        slot = leaving[BEHIND[kind]]
        mine = jnp.zeros((8, 128), I32)
        for b in range(KEPT):
            mine = jnp.where(sub == b, domain_key(codes[slot, b]) + slots[slot, b], mine)
        found = jnp.zeros((8, 128), I32)
        for a in range(KEPT):
            code = codes[slot, a]
            what = near_s[code, TYPES, slots[slot, a]]
            keys = near[code, pl.ds(what, 1), :] + domain_key(code)
            hit = (keys == mine) & (lane < KEPT)
            tile = jnp.where(hit, (code * TYPES + what + 1) * KEPT + lane, 0)
            found = jnp.where(lane == a, jnp.sum(tile, axis=1, keepdims=True), found)
        index_v[kind * KEPT : (kind + 1) * KEPT, :] = found
    to_scalars = pltpu.make_async_copy(index_v, index_s, local_sem.at[1])
    to_scalars.start()
    to_scalars.wait()

    second_tier(OVL)
    first_tier(DEN)
    left_rows(DEN)

    def middle(m, tiles):
        def one(j, carry):
            split_row(m, row_id(0, -1, 0) + j, tiles)
            return carry

        def sides(j, carry):
            split_row(m, row_id(1, -1, A) + j * TYPES, tiles)
            split_row(m, row_id(-1, -1, B) + j * TYPES, tiles)
            return carry

        lax.fori_loop(0, 3 * TYPES, one, 0)
        lax.fori_loop(0, 3, sides, 0)

    def third_tier(m, tiles):
        def one(j, carry):
            skip = lax.rem(j + 1, 3) * TYPES
            if m == DEN:
                for kind in (C, D):
                    landed(m, inner_ids + kind + skip)

                @pl.when(j == 1)
                def _():
                    landed(m, outer_id(1, D))

                @pl.when(j == 2)
                def _():
                    landed(m, outer_id(-1, C))

            for u, kinds in ((1, (B, C, D)), (-1, (A, C, D))):
                for kind in kinds:
                    which = row_id(u, -1, kind) + skip
                    if m == OVL or kind < C:
                        landed(m, which)
                    split_row(m, which, tiles)
            return carry

        lax.fori_loop(0, 3, one, 0)

    middle(OVL, tiles_s)
    third_tier(OVL, tiles_s)
    second_tier(DEN)

    ham_copies = []
    loads[5].wait()
    for kind in range(TYPES):
        ham_out[kind] = ham[leaving[kind]]
    for kind, (ux, uy) in enumerate(((1, 0), (-1, 0), (0, 1), (0, -1))):
        copy = pltpu.make_async_remote_copy(
            src_ref=ham_out.at[kind],
            dst_ref=ham_home.at[kind],
            send_sem=ham_send.at[kind],
            recv_sem=ham_recv.at[kind],
            device_id=beside(ux, uy),
            device_id_type=MESH,
        )
        copy.start()
        ham_copies.append(copy)

    product(0, tiles_s, to_left(1))
    middle(DEN, tiles_p)
    third_tier(DEN, tiles_p)
    product(1, tiles_p, to_left_and_second(0))
    product(0, tiles_s, to_left(1))

    def mixed_out(i, columns, v, total):
        m = 3.0 * second[i, :, columns] - 2.0 * v
        rim[MIX, own + i, :, columns] = m
        return total + folded(m * rim[OVL, own + i, :, columns])

    def mixed_along_y(i):
        for u in (1, -1):
            row_copy(MIX, own + i, row_id(0, -u, 0) + i, 0, u).start()

    def mixed_sent(i):
        for u in (1, -1):
            row_copy(MIX, own + i, row_id(-u, 0, 0) + i, u, 0).start()

        @pl.when(i < 2)
        def _():
            mixed_along_y(i)

    count = product(1, tiles_p, mixed_out, mixed_sent, jnp.zeros((8, 128), F32))

    def near_copy(s, j, mine):
        return pltpu.make_async_remote_copy(
            src_ref=near_sums.at[s, at_low],
            dst_ref=near_sums.at[s, mine],
            send_sem=sum_send.at[s, 0, j],
            recv_sem=sum_recv.at[s, 0, mine],
            device_id=near_peer(j),
            device_id_type=MESH,
        )

    def far_copy(s, j, mine):
        return pltpu.make_async_remote_copy(
            src_ref=far_sums.at[s, at_high],
            dst_ref=far_sums.at[s, mine],
            send_sem=sum_send.at[s, 1, j],
            recv_sem=sum_recv.at[s, 1, mine],
            device_id=far_peer(j),
            device_id_type=MESH,
        )

    def spread(copy_of, s, me, members):
        def step(o, carry):
            copy_of(s, (me + o) % members, me).start()
            return carry

        lax.fori_loop(1, members, step, 0)

    def collect(copy_of, s, me, members):
        def step(o, carry):
            j = (me + o) % members
            copy_of(s, j, j).wait_recv()
            return carry

        lax.fori_loop(1, members, step, 0)

    def sent(copy_of, s, me, members):
        def step(o, carry):
            copy_of(s, (me + o) % members, me).wait_send()
            return carry

        lax.fori_loop(1, members, step, 0)

    across = lax.broadcasted_iota(I32, (1, 128), 1)

    def over_all(tile):
        return jnp.sum(jnp.sum(tile, axis=0, keepdims=True), axis=1, keepdims=True)

    near_sums[0, at_low] = jnp.where(across < SIDE, over_all(start), over_all(count))
    spread(near_copy, 0, at_low, group)

    def pass_on(i):
        for dy in (-1, 1):
            arrive(MIX, 0, dy, i)
            for u in (1, -1):
                send(MIX, 0, dy, i, u, 0)

    collect(near_copy, 0, at_low, group)
    far_sums[0, at_high] = jnp.sum(near_sums[0], axis=0)
    spread(far_copy, 0, at_high, high)
    pass_on(0)
    pass_on(1)
    mixed_along_y(2)
    for u in (1, -1):
        if u == 1:
            landed(MIX, outer_id(0, 3))
        row_copy(MIX, outer_id(0, 3), outer_id(-u, 3), 0, u).start()
    mixed_along_y(3)
    collect(far_copy, 0, at_high, high)
    counts = jnp.sum(far_sums[0], axis=0)
    count_start = counts[:, :1]
    scale = count_start / counts[:, SIDE : SIDE + 1]
    left_rows(MIX, scale)
    pass_on(2)
    for dy in (-1, 1):
        arrive(MIX, 0, dy, 3)
        send_inner(MIX, dy, 3)
    product(0, tiles_s, to_left(1))

    def mixed_middle(j, carry):
        split_row(MIX, row_id(0, -1, 0) + j, tiles_p, scale)
        return carry

    def mixed_sides(j, carry):
        skip = lax.rem(j + 1, 3) * TYPES
        landed(MIX, inner_ids + 3 + skip)

        @pl.when(j > 0)
        def _():
            landed(MIX, outer_ids + 3 + skip)

        for kind in range(TYPES):
            for u in (1, -1):
                which = row_id(u, -1, kind) + skip
                if kind < 3:
                    landed(MIX, which)
                split_row(MIX, which, tiles_p, scale)
        return carry

    lax.fori_loop(0, 3 * TYPES, mixed_middle, 0)
    lax.fori_loop(0, 3, mixed_sides, 0)
    product(1, tiles_p, to_left_and_second(0))
    product(0, tiles_s, to_left(1))

    def last_out(i, columns, v, carry):
        total, largest = carry
        m = 3.0 * second[i, :, columns] - 2.0 * v
        last[i, :, columns] = m
        return (
            total + folded(m * rim[OVL, own + i, :, columns]),
            jnp.maximum(largest, jnp.max(jnp.abs(m).reshape(SIDE // 8, 8, 128), axis=0)),
        )

    zero = jnp.zeros((8, 128), F32)
    count, largest = product(1, tiles_p, last_out, None, (zero, zero))
    for copy in ham_copies:
        copy.wait_recv()
    largest = jnp.max(jnp.max(largest, axis=1, keepdims=True), axis=0, keepdims=True)
    size = jnp.where(largest > 1e-37, jnp.minimum(largest, 1e37), 1.0)
    inverse = 1.0 / size
    band = zero
    for i in range(TYPES):
        for k in range(COLUMNS // 128):
            columns = slice(k * 128, (k + 1) * 128)
            band += folded((last[i, :, columns] * inverse) * ham_home[i, :, columns])

    def joined(sums):
        biggest = jnp.max(sums, axis=0)
        ratio = pltpu.roll(sums, SIDE, 2) / pltpu.roll(biggest, SIDE, 1)[None]
        added = jnp.sum(jnp.where((across >= 32)[None], sums * ratio, sums), axis=0)
        return jnp.where(across < SIDE, added, biggest)

    near_sums[1, at_low] = jnp.where(
        across < 32, over_all(count), jnp.where(across < SIDE, over_all(band), size)
    )
    spread(near_copy, 1, at_low, group)
    collect(near_copy, 1, at_low, group)
    far_sums[1, at_high] = joined(near_sums[1])
    spread(far_copy, 1, at_high, high)
    collect(far_copy, 1, at_high, high)
    sums = joined(far_sums[1])
    scale = count_start / sums[:, :1]
    for slot in range(TYPES):
        out[0, 0, slot] = scale * last[near_s[4, TYPES, slot]]
    basis = nx * ny * TYPES * SIDE
    energy[0] = jnp.sum(sums[:, 32:33] * (sums[:, SIDE : SIDE + 1] * scale)) / basis

    for copy in (*near_copies, *ham_copies):
        copy.wait_send()

    first = {OVL: (row_id(1, 0, A), row_id(-1, 0, B), row_id(0, 1, C), row_id(0, -1, D))}
    first[DEN], first[MIX] = first[OVL], tuple(own + i for i in range(TYPES))
    for m in (OVL, DEN, MIX):
        for which in range(9 * TYPES):
            if which not in first[m]:
                row_copy(m, which, which, 1, 0).wait_send()
    for s in range(2):
        sent(near_copy, s, at_low, group)
        sent(far_copy, s, at_high, high)


def shards(nx, ny, ham, ovl, den, leaving, codes, slots):
    high, group = nx // LOW, LOW * ny
    vmem = pl.BlockSpec(memory_space=pltpu.VMEM)
    smem = pl.BlockSpec(memory_space=pltpu.SMEM)
    dma = pltpu.SemaphoreType.DMA
    purified, energy = pl.pallas_call(
        functools.partial(kernel, nx, ny),
        out_shape=(
            jax.ShapeDtypeStruct(den.shape, F32),
            jax.ShapeDtypeStruct((1,), F32),
        ),
        in_specs=[pl.BlockSpec(memory_space=pl.ANY)] * 6,
        out_specs=(vmem, smem),
        scratch_shapes=[
            *[pltpu.VMEM((TYPES, SIDE, COLUMNS), F32)] * 3,
            pltpu.SMEM((TYPES,), I32),
            pltpu.SMEM((TYPES, KEPT), I32),
            pltpu.SMEM((TYPES, KEPT), I32),
            pltpu.VMEM((3, 9 * TYPES, SIDE, COLUMNS), F32),
            pltpu.VMEM((TYPES, SIDE, COLUMNS), F32),
            pltpu.VMEM((TYPES, SIDE, COLUMNS), F32),
            pltpu.VMEM(((9 * TYPES + 1) * KEPT, SIDE, 128), BF16),
            pltpu.VMEM(((9 * TYPES + 1) * KEPT, SIDE, 128), BF16),
            pltpu.VMEM((2, TYPES, 2 * SIDE, COLUMNS), BF16),
            pltpu.VMEM((TYPES, SIDE, COLUMNS), F32),
            pltpu.VMEM((TYPES, SIDE, COLUMNS), F32),
            pltpu.VMEM((9, 8, 128), I32),
            pltpu.SMEM((9, 8, 128), I32),
            pltpu.VMEM((TYPES * KEPT, 128), I32),
            pltpu.SMEM((TYPES * KEPT, 128), I32),
            pltpu.VMEM((2, group, 1, 128), F32),
            pltpu.VMEM((2, high, 1, 128), F32),
            dma((3, 9 * TYPES)),
            dma((3, 9 * TYPES)),
            dma((TYPES,)),
            dma((TYPES,)),
            dma((9,)),
            dma((9,)),
            dma((2, 2, max(group, high))),
            dma((2, 2, max(group, high))),
            dma((2,)),
            dma((6,)),
        ],
        compiler_params=pltpu.CompilerParams(
            collective_id=0, has_side_effects=True, vmem_limit_bytes=60 * 1024 * 1024
        ),
    )(
        *(m.reshape(TYPES, SIDE, COLUMNS) for m in (ham, ovl, den)),
        leaving.reshape(TYPES), codes.reshape(TYPES, KEPT), slots.reshape(TYPES, KEPT),
    )
    return purified, energy.reshape(())


def solution(mesh):
    whole = P("gx", "gy", None, None, None)
    few = P("gx", "gy", None, None)
    return jax.shard_map(
        functools.partial(shards, mesh.shape["gx"], mesh.shape["gy"]),
        mesh=mesh,
        in_specs=(whole, whole, whole, few, few, few),
        out_specs=(whole, P()),
        check_vma=False,
    )
```

```python
import functools

import jax
import jax.numpy as jnp
from jax import lax
from jax.experimental import pallas as pl
from jax.experimental.pallas import tpu as pltpu
from jax.sharding import PartitionSpec as P

MESH = pl.DeviceIdType.MESH
F32, BF16, I32 = jnp.float32, jnp.bfloat16, jnp.int32
A, B, C, D = range(4)
SIDE, KEPT, TYPES = 64, 8, 4
COLUMNS = SIDE * KEPT
OVL, DEN, MIX = range(3)
BEHIND = (1, 0, 3, 2)
AROUND = [(ux, uy) for ux in (-1, 0, 1) for uy in (-1, 0, 1) if (ux, uy) != (0, 0)]
LOW = 4


def row_id(dx, dy, kind):
    return (3 * (dx + 1) + (dy + 1)) * TYPES + kind


def domain_key(code):
    across = (code * 11) >> 5
    return (across - 1) * 64 + (code - 3 * across - 1) * 8


def folded(tile):
    return jnp.sum(tile.reshape(tile.shape[0] // 8, 8, 128), axis=0)


def kernel(
    nx, ny,
    ham_hbm, ovl_hbm, den_hbm, leaving_hbm, codes_hbm, slots_hbm,
    out, energy,
    ham, ovl, den, leaving, codes, slots,
    rim, ham_out, ham_home, tiles_s, tiles_p, lhs, second, last,
    near, near_s, index_v, index_s, near_sums, far_sums,
    send_sem, recv_sem, ham_send, ham_recv, near_send, near_recv, sum_send, sum_recv, local_sem, load_sem,
):
    x, y = lax.axis_index("gx"), lax.axis_index("gy")
    high = nx // LOW
    group = LOW * ny
    at_high, at_low = x // LOW, (x % LOW) * ny + y

    def beside(ux, uy):
        return (lax.rem(x + ux + nx, nx), lax.rem(y + uy + ny, ny))

    def near_peer(j):
        return (at_high * LOW + j // ny, j % ny)

    def far_peer(j):
        return (j * LOW + x % LOW, y)

    loads = [
        pltpu.make_async_copy(there, here, load_sem.at[k])
        for k, (there, here) in enumerate((
            (leaving_hbm, leaving), (codes_hbm, codes), (slots_hbm, slots),
            (ovl_hbm, ovl), (den_hbm, den), (ham_hbm, ham),
        ))
    ]
    for load in loads:
        load.start()

    barrier = pltpu.get_barrier_semaphore()
    for ux, uy in AROUND:
        pl.semaphore_signal(barrier, inc=1, device_id=beside(ux, uy), device_id_type=MESH)

    def greet_near(o, carry):
        pl.semaphore_signal(barrier, inc=1, device_id=near_peer((at_low + o) % group), device_id_type=MESH)
        return carry

    def greet_far(o, carry):
        pl.semaphore_signal(barrier, inc=1, device_id=far_peer((at_high + o) % high), device_id_type=MESH)
        return carry

    lax.fori_loop(1, group, greet_near, 0)
    lax.fori_loop(1, high, greet_far, 0)

    lane = lax.broadcasted_iota(I32, (8, 128), 1)
    sub = lax.broadcasted_iota(I32, (8, 128), 0)

    for load in loads[:3]:
        load.wait()
    note = jnp.zeros((8, 128), I32)
    for kind in range(TYPES):
        slot = leaving[BEHIND[kind]]
        for c in range(KEPT):
            key = domain_key(codes[slot, c]) + slots[slot, c]
            note = jnp.where((sub == kind) & (lane == c), key, note)
        note = jnp.where((sub == TYPES) & (lane == slot), kind, note)
    near[4] = note

    for load in loads[3:5]:
        load.wait()
    start = jnp.zeros((8, 128), F32)
    for kind in range(TYPES):
        slot = leaving[kind]
        mine = row_id(*((1, 0), (-1, 0), (0, 1), (0, -1))[kind], kind)
        s_row, p_row = ovl[slot], den[slot]
        rim[OVL, mine] = s_row
        rim[DEN, mine] = p_row
        prod = s_row * p_row
        for k in range(COLUMNS // 128):
            start += folded(prod[:, k * 128 : (k + 1) * 128])

    pl.semaphore_wait(barrier, len(AROUND) + group - 1 + high - 1)

    def row_copy(m, which, there, ux, uy, left=None):
        return pltpu.make_async_remote_copy(
            src_ref=rim.at[m, which],
            dst_ref=rim.at[m, there],
            send_sem=send_sem.at[m, there if left is None else left],
            recv_sem=recv_sem.at[m, there],
            device_id=beside(ux, uy),
            device_id_type=MESH,
        )

    def send(m, dx, dy, kind, ux, uy):
        row_copy(m, row_id(dx, dy, kind), row_id(dx - ux, dy - uy, kind), ux, uy).start()

    def landed(m, which):
        row_copy(m, which, which, 1, 0).wait_recv()

    def arrive(m, dx, dy, kind):
        landed(m, row_id(dx, dy, kind))

    core = lax.rem(x, 2)
    outer, inner = 2 * core - 1, 1 - 2 * core
    outer_ids, inner_ids = core * (6 * TYPES), (1 - core) * (6 * TYPES)

    def outer_id(dy, kind):
        return outer_ids + ((dy + 1) * TYPES + kind)

    def send_inner(m, dy, kind):
        left = inner_ids + ((dy + 1) * TYPES + kind)
        row_copy(m, row_id(0, dy, kind), outer_id(dy, kind), inner, 0, left).start()

    def outer_on(m, dy, kind, uy):
        landed(m, outer_id(dy, kind))
        row_copy(m, outer_id(dy, kind), outer_id(dy - uy, kind), 0, uy).start()

    def start_y(m):
        send(m, 0, 1, C, 0, 1)
        send(m, 0, -1, D, 0, -1)
        for u in (1, -1):
            send(m, 1, 0, A, 0, u)
            send(m, -1, 0, B, 0, u)

    def start_x(m):
        send(m, 1, 0, A, 1, 0)
        send(m, -1, 0, B, -1, 0)
        for u in (1, -1):
            send(m, 0, 1, C, u, 0)
            send(m, 0, -1, D, u, 0)

    near_copies = []

    def tell_pattern():
        for k, (ux, uy) in enumerate(AROUND):
            there = row_id(-ux, -uy, 0) // TYPES
            copy = pltpu.make_async_remote_copy(
                src_ref=near.at[4],
                dst_ref=near.at[there],
                send_sem=near_send.at[there],
                recv_sem=near_recv.at[there],
                device_id=beside(ux, uy),
                device_id_type=MESH,
            )
            copy.start()
            near_copies.append(copy)

    tell_pattern()
    start_y(OVL)
    start_x(OVL)
    start_x(DEN)

    def first_tier(m):
        for kind, uy in ((C, 1), (D, -1)):
            arrive(m, 0, 0, kind)
            send(m, 0, 0, kind, 0, uy)
            if m == OVL:
                for u in (1, -1):
                    send(m, 0, 0, kind, u, 0)
            else:
                send_inner(m, 0, kind)
        arrive(m, 0, 0, A)
        send(m, 0, 0, A, 1, 0)
        arrive(m, 0, 0, B)
        send(m, 0, 0, B, -1, 0)
        for u in (1, -1):
            arrive(m, 1, u, A)
            send(m, 1, u, A, 1, 0)
            arrive(m, -1, u, B)
            send(m, -1, u, B, -1, 0)
        if m == DEN:
            outer_on(m, 0, C, 1)
            outer_on(m, 0, D, -1)

    def second_tier(m):
        for kind, uy in ((C, 1), (D, -1)):
            arrive(m, 0, -uy, kind)
            if m == OVL:
                for u in (1, -1):
                    send(m, 0, -uy, kind, u, 0)
            else:
                send_inner(m, -uy, kind)
        for u in (1, -1):
            arrive(m, 0, u, A)
            send(m, 0, u, A, 1, 0)
            arrive(m, 0, u, B)
            send(m, 0, u, B, -1, 0)

    half = lax.broadcasted_iota(I32, (SIDE, 128), 1) < SIDE

    def split_row(m, which, tiles, scale=None):
        for pair in range(KEPT // 2):
            v = rim[m, which, :, pair * 128 : (pair + 1) * 128]
            if scale is not None:
                v = v * scale
            top = v.astype(BF16)
            rest = pltpu.roll((v - top.astype(F32)).astype(BF16), SIDE, 1)
            tiles[(which + 1) * KEPT + 2 * pair] = jnp.where(half, top, rest)
            tiles[(which + 1) * KEPT + 2 * pair + 1] = jnp.where(half, rest, top)

    def split_left(into, i, columns, v):
        top = v.astype(BF16)
        lhs[into, i, 0:SIDE, columns] = top
        lhs[into, i, SIDE : 2 * SIDE, columns] = (v - top.astype(F32)).astype(BF16)

    def left_rows(m, scale=None):
        for i in range(TYPES):
            v = rim[m, row_id(0, 0, i)]
            split_left(0, i, slice(None), v if scale is None else v * scale)

    wide = lax.broadcasted_iota(I32, (SIDE, 128), 1) < SIDE

    def row_product(left, tiles, i, emit, carry=0):
        a = lhs[left, i]
        for pair in range(KEPT // 2):
            right = jnp.concatenate(
                [
                    jnp.concatenate([tiles[index_s[i * KEPT + b, e]] for e in range(KEPT)], axis=0)
                    for b in (2 * pair, 2 * pair + 1)
                ],
                axis=1,
            )
            full = jnp.dot(a, right, preferred_element_type=F32)
            both = full[:SIDE] + full[SIDE:]
            even, odd = both[:, :128], both[:, 128:]
            even = even + pltpu.roll(even, SIDE, 1)
            odd = odd + pltpu.roll(odd, SIDE, 1)
            carry = emit(i, slice(pair * 128, (pair + 1) * 128), jnp.where(wide, even, odd), carry)
        return carry

    def product(left, tiles, emit, carry=0):
        return lax.fori_loop(0, TYPES, lambda i, carry: row_product(left, tiles, i, emit, carry), carry)

    def to_left(into):
        def emit(i, columns, v, carry):
            split_left(into, i, columns, v)
            return carry

        return emit

    def to_left_and_second(into):
        def emit(i, columns, v, carry):
            split_left(into, i, columns, v)
            second[i, :, columns] = v
            return carry

        return emit

    own = row_id(0, 0, 0)

    for k in range(KEPT):
        tiles_s[k] = jnp.zeros((SIDE, 128), BF16)
        tiles_p[k] = jnp.zeros((SIDE, 128), BF16)
    first_tier(OVL)
    start_y(DEN)
    outer_on(DEN, 1, C, 1)
    outer_on(DEN, -1, D, -1)

    for copy in near_copies:
        copy.wait_recv()
    to_scalars = pltpu.make_async_copy(near, near_s, local_sem.at[0])
    to_scalars.start()
    to_scalars.wait()

    for kind in range(TYPES):
        slot = leaving[BEHIND[kind]]
        mine = jnp.zeros((8, 128), I32)
        for b in range(KEPT):
            mine = jnp.where(sub == b, domain_key(codes[slot, b]) + slots[slot, b], mine)
        found = jnp.zeros((8, 128), I32)
        for a in range(KEPT):
            code = codes[slot, a]
            what = near_s[code, TYPES, slots[slot, a]]
            keys = near[code, pl.ds(what, 1), :] + domain_key(code)
            hit = (keys == mine) & (lane < KEPT)
            tile = jnp.where(hit, (code * TYPES + what + 1) * KEPT + lane, 0)
            found = jnp.where(lane == a, jnp.sum(tile, axis=1, keepdims=True), found)
        index_v[kind * KEPT : (kind + 1) * KEPT, :] = found
    to_scalars = pltpu.make_async_copy(index_v, index_s, local_sem.at[1])
    to_scalars.start()
    to_scalars.wait()

    second_tier(OVL)
    first_tier(DEN)
    left_rows(DEN)

    def middle(m, tiles):
        def one(j, carry):
            split_row(m, row_id(0, -1, 0) + j, tiles)
            return carry

        def sides(j, carry):
            split_row(m, row_id(1, -1, A) + j * TYPES, tiles)
            split_row(m, row_id(-1, -1, B) + j * TYPES, tiles)
            return carry

        lax.fori_loop(0, 3 * TYPES, one, 0)
        lax.fori_loop(0, 3, sides, 0)

    def third_tier(m, tiles):
        def one(j, carry):
            skip = lax.rem(j + 1, 3) * TYPES
            if m == DEN:
                for kind in (C, D):
                    landed(m, inner_ids + kind + skip)

                @pl.when(j == 1)
                def _():
                    landed(m, outer_id(1, D))

                @pl.when(j == 2)
                def _():
                    landed(m, outer_id(-1, C))

            for u, kinds in ((1, (B, C, D)), (-1, (A, C, D))):
                for kind in kinds:
                    which = row_id(u, -1, kind) + skip
                    if m == OVL or kind < C:
                        landed(m, which)
                    split_row(m, which, tiles)
            return carry

        lax.fori_loop(0, 3, one, 0)

    middle(OVL, tiles_s)
    third_tier(OVL, tiles_s)
    second_tier(DEN)

    ham_copies = []
    loads[5].wait()
    for kind in range(TYPES):
        ham_out[kind] = ham[leaving[kind]]
    for kind, (ux, uy) in enumerate(((1, 0), (-1, 0), (0, 1), (0, -1))):
        copy = pltpu.make_async_remote_copy(
            src_ref=ham_out.at[kind],
            dst_ref=ham_home.at[kind],
            send_sem=ham_send.at[kind],
            recv_sem=ham_recv.at[kind],
            device_id=beside(ux, uy),
            device_id_type=MESH,
        )
        copy.start()
        ham_copies.append(copy)

    product(0, tiles_s, to_left(1))
    middle(DEN, tiles_p)
    third_tier(DEN, tiles_p)

    def mixed_out(i, columns, v, total):
        m = 3.0 * second[i, :, columns] - 2.0 * v
        rim[MIX, own + i, :, columns] = m
        return total + folded(m * rim[OVL, own + i, :, columns])

    def mixed_along_y(i):
        for u in (1, -1):
            row_copy(MIX, own + i, row_id(0, -u, 0) + i, 0, u).start()

    def mixed_sent(i):
        for u in (1, -1):
            row_copy(MIX, own + i, row_id(-u, 0, 0) + i, u, 0).start()

        @pl.when(i < 2)
        def _():
            mixed_along_y(i)

    def one_row(i, total):
        row_product(1, tiles_p, i, to_left_and_second(0))
        row_product(0, tiles_s, i, to_left(1))
        total = row_product(1, tiles_p, i, mixed_out, total)
        mixed_sent(i)
        return total

    count = lax.fori_loop(0, TYPES, one_row, jnp.zeros((8, 128), F32))

    def near_copy(s, j, mine):
        return pltpu.make_async_remote_copy(
            src_ref=near_sums.at[s, at_low],
            dst_ref=near_sums.at[s, mine],
            send_sem=sum_send.at[s, 0, j],
            recv_sem=sum_recv.at[s, 0, mine],
            device_id=near_peer(j),
            device_id_type=MESH,
        )

    def far_copy(s, j, mine):
        return pltpu.make_async_remote_copy(
            src_ref=far_sums.at[s, at_high],
            dst_ref=far_sums.at[s, mine],
            send_sem=sum_send.at[s, 1, j],
            recv_sem=sum_recv.at[s, 1, mine],
            device_id=far_peer(j),
            device_id_type=MESH,
        )

    def spread(copy_of, s, me, members):
        def step(o, carry):
            copy_of(s, (me + o) % members, me).start()
            return carry

        lax.fori_loop(1, members, step, 0, unroll=True)

    def collect(copy_of, s, me, members):
        def step(o, carry):
            j = (me + o) % members
            copy_of(s, j, j).wait_recv()
            return carry

        lax.fori_loop(1, members, step, 0, unroll=True)

    def sent(copy_of, s, me, members):
        def step(o, carry):
            copy_of(s, (me + o) % members, me).wait_send()
            return carry

        lax.fori_loop(1, members, step, 0)

    across = lax.broadcasted_iota(I32, (1, 128), 1)

    def over_all(tile):
        return jnp.sum(jnp.sum(tile, axis=0, keepdims=True), axis=1, keepdims=True)

    near_sums[0, at_low] = jnp.where(across < SIDE, over_all(start), over_all(count))
    spread(near_copy, 0, at_low, group)

    def pass_on(i):
        for dy in (-1, 1):
            arrive(MIX, 0, dy, i)
            for u in (1, -1):
                send(MIX, 0, dy, i, u, 0)

    pass_on(0)
    mixed_along_y(2)
    collect(near_copy, 0, at_low, group)
    far_sums[0, at_high] = jnp.sum(near_sums[0], axis=0)
    spread(far_copy, 0, at_high, high)
    pass_on(1)
    mixed_along_y(3)
    pass_on(2)
    for u in (1, -1):
        if u == 1:
            landed(MIX, outer_id(0, 3))
        row_copy(MIX, outer_id(0, 3), outer_id(-u, 3), 0, u).start()
    collect(far_copy, 0, at_high, high)
    counts = jnp.sum(far_sums[0], axis=0)
    count_start = counts[:, :1]
    scale = count_start / counts[:, SIDE : SIDE + 1]
    left_rows(MIX, scale)
    for dy in (-1, 1):
        arrive(MIX, 0, dy, 3)
        send_inner(MIX, dy, 3)
    product(0, tiles_s, to_left(1))

    def mixed_middle(j, carry):
        split_row(MIX, row_id(0, -1, 0) + j, tiles_p, scale)
        return carry

    def mixed_sides(j, carry):
        skip = lax.rem(j + 1, 3) * TYPES
        landed(MIX, inner_ids + 3 + skip)

        @pl.when(j > 0)
        def _():
            landed(MIX, outer_ids + 3 + skip)

        for kind in range(TYPES):
            for u in (1, -1):
                which = row_id(u, -1, kind) + skip
                if kind < 3:
                    landed(MIX, which)
                split_row(MIX, which, tiles_p, scale)
        return carry

    lax.fori_loop(0, 3 * TYPES, mixed_middle, 0)
    lax.fori_loop(0, 3, mixed_sides, 0)
    product(1, tiles_p, to_left_and_second(0))
    product(0, tiles_s, to_left(1))

    def last_out(i, columns, v, carry):
        total, largest = carry
        m = 3.0 * second[i, :, columns] - 2.0 * v
        last[i, :, columns] = m
        return (
            total + folded(m * rim[OVL, own + i, :, columns]),
            jnp.maximum(largest, jnp.max(jnp.abs(m).reshape(SIDE // 8, 8, 128), axis=0)),
        )

    zero = jnp.zeros((8, 128), F32)
    count, largest = product(1, tiles_p, last_out, (zero, zero))
    for copy in ham_copies:
        copy.wait_recv()
    largest = jnp.max(jnp.max(largest, axis=1, keepdims=True), axis=0, keepdims=True)
    size = jnp.where(largest > 1e-37, jnp.minimum(largest, 1e37), 1.0)
    inverse = 1.0 / size
    band = zero
    for i in range(TYPES):
        for k in range(COLUMNS // 128):
            columns = slice(k * 128, (k + 1) * 128)
            band += folded((last[i, :, columns] * inverse) * ham_home[i, :, columns])

    def joined(sums):
        biggest = jnp.max(sums, axis=0)
        ratio = pltpu.roll(sums, SIDE, 2) / pltpu.roll(biggest, SIDE, 1)[None]
        added = jnp.sum(jnp.where((across >= 32)[None], sums * ratio, sums), axis=0)
        return jnp.where(across < SIDE, added, biggest)

    near_sums[1, at_low] = jnp.where(
        across < 32, over_all(count), jnp.where(across < SIDE, over_all(band), size)
    )
    spread(near_copy, 1, at_low, group)
    for copy in (*near_copies, *ham_copies):
        copy.wait_send()

    first = {OVL: (row_id(1, 0, A), row_id(-1, 0, B), row_id(0, 1, C), row_id(0, -1, D))}
    first[DEN], first[MIX] = first[OVL], tuple(own + i for i in range(TYPES))
    for m in (OVL, DEN, MIX):
        for which in range(9 * TYPES):
            if which not in first[m]:
                row_copy(m, which, which, 1, 0).wait_send()
    sent(near_copy, 0, at_low, group)
    sent(far_copy, 0, at_high, high)
    collect(near_copy, 1, at_low, group)
    far_sums[1, at_high] = joined(near_sums[1])
    spread(far_copy, 1, at_high, high)
    collect(far_copy, 1, at_high, high)
    sums = joined(far_sums[1])
    scale = count_start / sums[:, :1]
    for slot in range(TYPES):
        out[0, 0, slot] = scale * last[near_s[4, TYPES, slot]]
    basis = nx * ny * TYPES * SIDE
    energy[0] = jnp.sum(sums[:, 32:33] * (sums[:, SIDE : SIDE + 1] * scale)) / basis

    sent(near_copy, 1, at_low, group)
    sent(far_copy, 1, at_high, high)


def shards(nx, ny, ham, ovl, den, leaving, codes, slots):
    high, group = nx // LOW, LOW * ny
    vmem = pl.BlockSpec(memory_space=pltpu.VMEM)
    smem = pl.BlockSpec(memory_space=pltpu.SMEM)
    dma = pltpu.SemaphoreType.DMA
    purified, energy = pl.pallas_call(
        functools.partial(kernel, nx, ny),
        out_shape=(
            jax.ShapeDtypeStruct(den.shape, F32),
            jax.ShapeDtypeStruct((1,), F32),
        ),
        in_specs=[pl.BlockSpec(memory_space=pl.ANY)] * 6,
        out_specs=(vmem, smem),
        scratch_shapes=[
            *[pltpu.VMEM((TYPES, SIDE, COLUMNS), F32)] * 3,
            pltpu.SMEM((TYPES,), I32),
            pltpu.SMEM((TYPES, KEPT), I32),
            pltpu.SMEM((TYPES, KEPT), I32),
            pltpu.VMEM((3, 9 * TYPES, SIDE, COLUMNS), F32),
            pltpu.VMEM((TYPES, SIDE, COLUMNS), F32),
            pltpu.VMEM((TYPES, SIDE, COLUMNS), F32),
            pltpu.VMEM(((9 * TYPES + 1) * KEPT, SIDE, 128), BF16),
            pltpu.VMEM(((9 * TYPES + 1) * KEPT, SIDE, 128), BF16),
            pltpu.VMEM((2, TYPES, 2 * SIDE, COLUMNS), BF16),
            pltpu.VMEM((TYPES, SIDE, COLUMNS), F32),
            pltpu.VMEM((TYPES, SIDE, COLUMNS), F32),
            pltpu.VMEM((9, 8, 128), I32),
            pltpu.SMEM((9, 8, 128), I32),
            pltpu.VMEM((TYPES * KEPT, 128), I32),
            pltpu.SMEM((TYPES * KEPT, 128), I32),
            pltpu.VMEM((2, group, 1, 128), F32),
            pltpu.VMEM((2, high, 1, 128), F32),
            dma((3, 9 * TYPES)),
            dma((3, 9 * TYPES)),
            dma((TYPES,)),
            dma((TYPES,)),
            dma((9,)),
            dma((9,)),
            dma((2, 2, max(group, high))),
            dma((2, 2, max(group, high))),
            dma((2,)),
            dma((6,)),
        ],
        compiler_params=pltpu.CompilerParams(
            collective_id=0, has_side_effects=True, vmem_limit_bytes=60 * 1024 * 1024
        ),
    )(
        *(m.reshape(TYPES, SIDE, COLUMNS) for m in (ham, ovl, den)),
        leaving.reshape(TYPES), codes.reshape(TYPES, KEPT), slots.reshape(TYPES, KEPT),
    )
    return purified, energy.reshape(())


def solution(mesh):
    whole = P("gx", "gy", None, None, None)
    few = P("gx", "gy", None, None)
    return jax.shard_map(
        functools.partial(shards, mesh.shape["gx"], mesh.shape["gy"]),
        mesh=mesh,
        in_specs=(whole, whole, whole, few, few, few),
        out_specs=(whole, P()),
        check_vma=False,
    )
```

```python
import functools

import jax
import jax.numpy as jnp
from jax import lax
from jax.experimental import pallas as pl
from jax.experimental.pallas import tpu as pltpu
from jax.sharding import PartitionSpec as P

MESH = pl.DeviceIdType.MESH
F32, BF16, I32 = jnp.float32, jnp.bfloat16, jnp.int32
A, B, C, D = range(4)
SIDE, KEPT, TYPES = 64, 8, 4
COLUMNS = SIDE * KEPT
OVL, DEN, MIX = range(3)
BEHIND = (1, 0, 3, 2)
AROUND = [(ux, uy) for ux in (-1, 0, 1) for uy in (-1, 0, 1) if (ux, uy) != (0, 0)]
LOW = 4


def row_id(dx, dy, kind):
    return (3 * (dx + 1) + (dy + 1)) * TYPES + kind


def domain_key(code):
    across = (code * 11) >> 5
    return (across - 1) * 64 + (code - 3 * across - 1) * 8


def folded(tile):
    return jnp.sum(tile.reshape(tile.shape[0] // 8, 8, 128), axis=0)


def kernel(
    nx, ny,
    ham_hbm, ovl_hbm, den_hbm, leaving_hbm, codes_hbm, slots_hbm,
    out, energy,
    ham, ovl, den, leaving, codes, slots,
    rim, ham_out, ham_home, tiles_s, tiles_p, lhs, second, last,
    near, near_s, index_v, index_s, near_sums, far_sums,
    send_sem, recv_sem, ham_send, ham_recv, near_send, near_recv, sum_send, sum_recv, local_sem, load_sem,
):
    x, y = lax.axis_index("gx"), lax.axis_index("gy")
    high = nx // LOW
    group = LOW * ny
    at_high, at_low = x // LOW, (x % LOW) * ny + y

    def beside(ux, uy):
        return (lax.rem(x + ux + nx, nx), lax.rem(y + uy + ny, ny))

    def near_peer(j):
        return (at_high * LOW + j // ny, j % ny)

    def far_peer(j):
        return (j * LOW + x % LOW, y)

    loads = [
        pltpu.make_async_copy(there, here, load_sem.at[k])
        for k, (there, here) in enumerate((
            (leaving_hbm, leaving), (codes_hbm, codes), (slots_hbm, slots),
            (ovl_hbm, ovl), (den_hbm, den), (ham_hbm, ham),
        ))
    ]
    for load in loads:
        load.start()

    barrier = pltpu.get_barrier_semaphore()
    for ux, uy in AROUND:
        pl.semaphore_signal(barrier, inc=1, device_id=beside(ux, uy), device_id_type=MESH)

    def greet_near(o, carry):
        pl.semaphore_signal(barrier, inc=1, device_id=near_peer((at_low + o) % group), device_id_type=MESH)
        return carry

    def greet_far(o, carry):
        pl.semaphore_signal(barrier, inc=1, device_id=far_peer((at_high + o) % high), device_id_type=MESH)
        return carry

    lax.fori_loop(1, group, greet_near, 0)
    lax.fori_loop(1, high, greet_far, 0)

    lane = lax.broadcasted_iota(I32, (8, 128), 1)
    sub = lax.broadcasted_iota(I32, (8, 128), 0)

    for load in loads[:3]:
        load.wait()
    note = jnp.zeros((8, 128), I32)
    for kind in range(TYPES):
        slot = leaving[BEHIND[kind]]
        for c in range(KEPT):
            key = domain_key(codes[slot, c]) + slots[slot, c]
            note = jnp.where((sub == kind) & (lane == c), key, note)
        note = jnp.where((sub == TYPES) & (lane == slot), kind, note)
    near[4] = note

    for load in loads[3:5]:
        load.wait()
    start = jnp.zeros((8, 128), F32)
    for kind in range(TYPES):
        slot = leaving[kind]
        mine = row_id(*((1, 0), (-1, 0), (0, 1), (0, -1))[kind], kind)
        s_row, p_row = ovl[slot], den[slot]
        rim[OVL, mine] = s_row
        rim[DEN, mine] = p_row
        prod = s_row * p_row
        for k in range(COLUMNS // 128):
            start += folded(prod[:, k * 128 : (k + 1) * 128])

    pl.semaphore_wait(barrier, len(AROUND) + group - 1 + high - 1)

    def row_copy(m, which, there, ux, uy, left=None):
        return pltpu.make_async_remote_copy(
            src_ref=rim.at[m, which],
            dst_ref=rim.at[m, there],
            send_sem=send_sem.at[m, there if left is None else left],
            recv_sem=recv_sem.at[m, there],
            device_id=beside(ux, uy),
            device_id_type=MESH,
        )

    def send(m, dx, dy, kind, ux, uy):
        row_copy(m, row_id(dx, dy, kind), row_id(dx - ux, dy - uy, kind), ux, uy).start()

    def landed(m, which):
        row_copy(m, which, which, 1, 0).wait_recv()

    def arrive(m, dx, dy, kind):
        landed(m, row_id(dx, dy, kind))

    core = lax.rem(x, 2)
    outer, inner = 2 * core - 1, 1 - 2 * core
    outer_ids, inner_ids = core * (6 * TYPES), (1 - core) * (6 * TYPES)

    def outer_id(dy, kind):
        return outer_ids + ((dy + 1) * TYPES + kind)

    def send_inner(m, dy, kind):
        left = inner_ids + ((dy + 1) * TYPES + kind)
        row_copy(m, row_id(0, dy, kind), outer_id(dy, kind), inner, 0, left).start()

    def outer_on(m, dy, kind, uy):
        landed(m, outer_id(dy, kind))
        row_copy(m, outer_id(dy, kind), outer_id(dy - uy, kind), 0, uy).start()

    def start_y(m):
        send(m, 0, 1, C, 0, 1)
        send(m, 0, -1, D, 0, -1)
        for u in (1, -1):
            send(m, 1, 0, A, 0, u)
            send(m, -1, 0, B, 0, u)

    def start_x(m):
        send(m, 1, 0, A, 1, 0)
        send(m, -1, 0, B, -1, 0)
        for u in (1, -1):
            send(m, 0, 1, C, u, 0)
            send(m, 0, -1, D, u, 0)

    near_copies = []

    def tell_pattern():
        for k, (ux, uy) in enumerate(AROUND):
            there = row_id(-ux, -uy, 0) // TYPES
            copy = pltpu.make_async_remote_copy(
                src_ref=near.at[4],
                dst_ref=near.at[there],
                send_sem=near_send.at[there],
                recv_sem=near_recv.at[there],
                device_id=beside(ux, uy),
                device_id_type=MESH,
            )
            copy.start()
            near_copies.append(copy)

    tell_pattern()
    start_x(OVL)
    start_y(OVL)
    start_x(DEN)

    def first_tier(m):
        for kind, uy in ((C, 1), (D, -1)):
            arrive(m, 0, 0, kind)
            send(m, 0, 0, kind, 0, uy)
            if m == OVL:
                for u in (1, -1):
                    send(m, 0, 0, kind, u, 0)
            else:
                send_inner(m, 0, kind)
        arrive(m, 0, 0, A)
        send(m, 0, 0, A, 1, 0)
        arrive(m, 0, 0, B)
        send(m, 0, 0, B, -1, 0)
        for u in (1, -1):
            arrive(m, 1, u, A)
            send(m, 1, u, A, 1, 0)
            arrive(m, -1, u, B)
            send(m, -1, u, B, -1, 0)
        if m == DEN:
            outer_on(m, 0, C, 1)
            outer_on(m, 0, D, -1)

    def second_tier(m):
        for kind, uy in ((C, 1), (D, -1)):
            arrive(m, 0, -uy, kind)
            if m == OVL:
                for u in (1, -1):
                    send(m, 0, -uy, kind, u, 0)
            else:
                send_inner(m, -uy, kind)
        for u in (1, -1):
            arrive(m, 0, u, A)
            send(m, 0, u, A, 1, 0)
            arrive(m, 0, u, B)
            send(m, 0, u, B, -1, 0)

    half = lax.broadcasted_iota(I32, (SIDE, 128), 1) < SIDE

    def split_row(m, which, tiles, scale=None):
        for pair in range(KEPT // 2):
            v = rim[m, which, :, pair * 128 : (pair + 1) * 128]
            if scale is not None:
                v = v * scale
            top = v.astype(BF16)
            rest = pltpu.roll((v - top.astype(F32)).astype(BF16), SIDE, 1)
            tiles[(which + 1) * KEPT + 2 * pair] = jnp.where(half, top, rest)
            tiles[(which + 1) * KEPT + 2 * pair + 1] = jnp.where(half, rest, top)

    def split_left(into, i, columns, v):
        top = v.astype(BF16)
        lhs[into, i, 0:SIDE, columns] = top
        lhs[into, i, SIDE : 2 * SIDE, columns] = (v - top.astype(F32)).astype(BF16)

    def left_rows(m, scale=None):
        for i in range(TYPES):
            v = rim[m, row_id(0, 0, i)]
            split_left(0, i, slice(None), v if scale is None else v * scale)

    wide = lax.broadcasted_iota(I32, (SIDE, 128), 1) < SIDE

    def row_product(left, tiles, i, emit, carry=0):
        a = lhs[left, i]
        for pair in range(KEPT // 2):
            right = jnp.concatenate(
                [
                    jnp.concatenate([tiles[index_s[i * KEPT + b, e]] for e in range(KEPT)], axis=0)
                    for b in (2 * pair, 2 * pair + 1)
                ],
                axis=1,
            )
            full = jnp.dot(a, right, preferred_element_type=F32)
            both = full[:SIDE] + full[SIDE:]
            even, odd = both[:, :128], both[:, 128:]
            even = even + pltpu.roll(even, SIDE, 1)
            odd = odd + pltpu.roll(odd, SIDE, 1)
            carry = emit(i, slice(pair * 128, (pair + 1) * 128), jnp.where(wide, even, odd), carry)
        return carry

    def product(left, tiles, emit, carry=0):
        return lax.fori_loop(0, TYPES, lambda i, carry: row_product(left, tiles, i, emit, carry), carry, unroll=True)

    def to_left(into):
        def emit(i, columns, v, carry):
            split_left(into, i, columns, v)
            return carry

        return emit

    def to_left_and_second(into):
        def emit(i, columns, v, carry):
            split_left(into, i, columns, v)
            second[i, :, columns] = v
            return carry

        return emit

    own = row_id(0, 0, 0)

    for k in range(KEPT):
        tiles_s[k] = jnp.zeros((SIDE, 128), BF16)
        tiles_p[k] = jnp.zeros((SIDE, 128), BF16)
    first_tier(OVL)
    start_y(DEN)
    outer_on(DEN, 1, C, 1)
    outer_on(DEN, -1, D, -1)

    for copy in near_copies:
        copy.wait_recv()
    to_scalars = pltpu.make_async_copy(near, near_s, local_sem.at[0])
    to_scalars.start()
    to_scalars.wait()

    for kind in range(TYPES):
        slot = leaving[BEHIND[kind]]
        mine = jnp.zeros((8, 128), I32)
        for b in range(KEPT):
            mine = jnp.where(sub == b, domain_key(codes[slot, b]) + slots[slot, b], mine)
        found = jnp.zeros((8, 128), I32)
        for a in range(KEPT):
            code = codes[slot, a]
            what = near_s[code, TYPES, slots[slot, a]]
            keys = near[code, pl.ds(what, 1), :] + domain_key(code)
            hit = (keys == mine) & (lane < KEPT)
            tile = jnp.where(hit, (code * TYPES + what + 1) * KEPT + lane, 0)
            found = jnp.where(lane == a, jnp.sum(tile, axis=1, keepdims=True), found)
        index_v[kind * KEPT : (kind + 1) * KEPT, :] = found
    to_scalars = pltpu.make_async_copy(index_v, index_s, local_sem.at[1])
    to_scalars.start()
    to_scalars.wait()

    second_tier(OVL)
    first_tier(DEN)
    left_rows(DEN)

    def middle(m, tiles):
        def one(j, carry):
            split_row(m, row_id(0, -1, 0) + j, tiles)
            return carry

        def sides(j, carry):
            split_row(m, row_id(1, -1, A) + j * TYPES, tiles)
            split_row(m, row_id(-1, -1, B) + j * TYPES, tiles)
            return carry

        lax.fori_loop(0, 3 * TYPES, one, 0)
        lax.fori_loop(0, 3, sides, 0)

    def third_tier(m, tiles):
        def one(j, carry):
            skip = lax.rem(j + 1, 3) * TYPES
            if m == DEN:
                for kind in (C, D):
                    landed(m, inner_ids + kind + skip)

                @pl.when(j == 1)
                def _():
                    landed(m, outer_id(1, D))

                @pl.when(j == 2)
                def _():
                    landed(m, outer_id(-1, C))

            for u, kinds in ((1, (B, C, D)), (-1, (A, C, D))):
                for kind in kinds:
                    which = row_id(u, -1, kind) + skip
                    if m == OVL or kind < C:
                        landed(m, which)
                    split_row(m, which, tiles)
            return carry

        lax.fori_loop(0, 3, one, 0)

    middle(OVL, tiles_s)
    third_tier(OVL, tiles_s)
    second_tier(DEN)

    ham_copies = []
    loads[5].wait()
    for kind in range(TYPES):
        ham_out[kind] = ham[leaving[kind]]
    for kind, (ux, uy) in enumerate(((1, 0), (-1, 0), (0, 1), (0, -1))):
        copy = pltpu.make_async_remote_copy(
            src_ref=ham_out.at[kind],
            dst_ref=ham_home.at[kind],
            send_sem=ham_send.at[kind],
            recv_sem=ham_recv.at[kind],
            device_id=beside(ux, uy),
            device_id_type=MESH,
        )
        copy.start()
        ham_copies.append(copy)

    product(0, tiles_s, to_left(1))
    middle(DEN, tiles_p)
    third_tier(DEN, tiles_p)

    def mixed_out(i, columns, v, total):
        m = 3.0 * second[i, :, columns] - 2.0 * v
        rim[MIX, own + i, :, columns] = m
        return total + folded(m * rim[OVL, own + i, :, columns])

    def mixed_along_y(i):
        for u in (1, -1):
            row_copy(MIX, own + i, row_id(0, -u, 0) + i, 0, u).start()

    def mixed_sent(i):
        for u in (1, -1):
            row_copy(MIX, own + i, row_id(-u, 0, 0) + i, u, 0).start()

        @pl.when(i < 2)
        def _():
            mixed_along_y(i)

    def one_row(i, total):
        row_product(1, tiles_p, i, to_left_and_second(0))
        row_product(0, tiles_s, i, to_left(1))
        total = row_product(1, tiles_p, i, mixed_out, total)
        mixed_sent(i)
        return total

    count = lax.fori_loop(0, TYPES, one_row, jnp.zeros((8, 128), F32))

    def near_copy(s, j, mine):
        return pltpu.make_async_remote_copy(
            src_ref=near_sums.at[s, at_low],
            dst_ref=near_sums.at[s, mine],
            send_sem=sum_send.at[s, 0, j],
            recv_sem=sum_recv.at[s, 0, mine],
            device_id=near_peer(j),
            device_id_type=MESH,
        )

    def far_copy(s, j, mine):
        return pltpu.make_async_remote_copy(
            src_ref=far_sums.at[s, at_high],
            dst_ref=far_sums.at[s, mine],
            send_sem=sum_send.at[s, 1, j],
            recv_sem=sum_recv.at[s, 1, mine],
            device_id=far_peer(j),
            device_id_type=MESH,
        )

    def spread(copy_of, s, me, members):
        def step(o, carry):
            copy_of(s, (me + o) % members, me).start()
            return carry

        lax.fori_loop(1, members, step, 0, unroll=True)

    def collect(copy_of, s, me, members):
        def step(o, carry):
            j = (me + o) % members
            copy_of(s, j, j).wait_recv()
            return carry

        lax.fori_loop(1, members, step, 0, unroll=True)

    def sent(copy_of, s, me, members):
        def step(o, carry):
            copy_of(s, (me + o) % members, me).wait_send()
            return carry

        lax.fori_loop(1, members, step, 0)

    across = lax.broadcasted_iota(I32, (1, 128), 1)

    def over_all(tile):
        return jnp.sum(jnp.sum(tile, axis=0, keepdims=True), axis=1, keepdims=True)

    near_sums[0, at_low] = jnp.where(across < SIDE, over_all(start), over_all(count))
    spread(near_copy, 0, at_low, group)

    def pass_on(i):
        for dy in (-1, 1):
            arrive(MIX, 0, dy, i)
            for u in (1, -1):
                send(MIX, 0, dy, i, u, 0)

    pass_on(0)
    mixed_along_y(2)
    collect(near_copy, 0, at_low, group)
    far_sums[0, at_high] = jnp.sum(near_sums[0], axis=0)
    spread(far_copy, 0, at_high, high)
    pass_on(1)
    mixed_along_y(3)
    pass_on(2)
    for u in (1, -1):
        if u == 1:
            landed(MIX, outer_id(0, 3))
        row_copy(MIX, outer_id(0, 3), outer_id(-u, 3), 0, u).start()
    collect(far_copy, 0, at_high, high)
    counts = jnp.sum(far_sums[0], axis=0)
    count_start = counts[:, :1]
    scale = count_start / counts[:, SIDE : SIDE + 1]
    left_rows(MIX, scale)
    for dy in (-1, 1):
        arrive(MIX, 0, dy, 3)
        send_inner(MIX, dy, 3)
    product(0, tiles_s, to_left(1))

    def mixed_middle(j, carry):
        split_row(MIX, row_id(0, -1, 0) + j, tiles_p, scale)
        return carry

    def mixed_sides(j, carry):
        skip = lax.rem(j + 1, 3) * TYPES
        landed(MIX, inner_ids + 3 + skip)

        @pl.when(j > 0)
        def _():
            landed(MIX, outer_ids + 3 + skip)

        for kind in range(TYPES):
            for u in (1, -1):
                which = row_id(u, -1, kind) + skip
                if kind < 3:
                    landed(MIX, which)
                split_row(MIX, which, tiles_p, scale)
        return carry

    lax.fori_loop(0, 3 * TYPES, mixed_middle, 0)
    lax.fori_loop(0, 3, mixed_sides, 0)
    product(1, tiles_p, to_left_and_second(0))
    product(0, tiles_s, to_left(1))

    def last_out(i, columns, v, carry):
        total, largest = carry
        m = 3.0 * second[i, :, columns] - 2.0 * v
        last[i, :, columns] = m
        return (
            total + folded(m * rim[OVL, own + i, :, columns]),
            jnp.maximum(largest, jnp.max(jnp.abs(m).reshape(SIDE // 8, 8, 128), axis=0)),
        )

    zero = jnp.zeros((8, 128), F32)
    count, largest = product(1, tiles_p, last_out, (zero, zero))
    for copy in ham_copies:
        copy.wait_recv()
    largest = jnp.max(jnp.max(largest, axis=1, keepdims=True), axis=0, keepdims=True)
    size = jnp.where(largest > 1e-37, jnp.minimum(largest, 1e37), 1.0)
    inverse = 1.0 / size
    band = zero
    for i in range(TYPES):
        for k in range(COLUMNS // 128):
            columns = slice(k * 128, (k + 1) * 128)
            band += folded((last[i, :, columns] * inverse) * ham_home[i, :, columns])

    def joined(sums):
        biggest = jnp.max(sums, axis=0)
        ratio = pltpu.roll(sums, SIDE, 2) / pltpu.roll(biggest, SIDE, 1)[None]
        added = jnp.sum(jnp.where((across >= 32)[None], sums * ratio, sums), axis=0)
        return jnp.where(across < SIDE, added, biggest)

    near_sums[1, at_low] = jnp.where(
        across < 32, over_all(count), jnp.where(across < SIDE, over_all(band), size)
    )
    spread(near_copy, 1, at_low, group)
    for copy in (*near_copies, *ham_copies):
        copy.wait_send()

    first = {OVL: (row_id(1, 0, A), row_id(-1, 0, B), row_id(0, 1, C), row_id(0, -1, D))}
    first[DEN], first[MIX] = first[OVL], tuple(own + i for i in range(TYPES))
    for m in (OVL, DEN, MIX):
        for which in range(9 * TYPES):
            if which not in first[m]:
                row_copy(m, which, which, 1, 0).wait_send()
    sent(near_copy, 0, at_low, group)
    sent(far_copy, 0, at_high, high)
    collect(near_copy, 1, at_low, group)
    far_sums[1, at_high] = joined(near_sums[1])
    spread(far_copy, 1, at_high, high)
    collect(far_copy, 1, at_high, high)
    sums = joined(far_sums[1])
    scale = count_start / sums[:, :1]
    for slot in range(TYPES):
        out[0, 0, slot] = scale * last[near_s[4, TYPES, slot]]
    basis = nx * ny * TYPES * SIDE
    energy[0] = jnp.sum(sums[:, 32:33] * (sums[:, SIDE : SIDE + 1] * scale)) / basis

    sent(near_copy, 1, at_low, group)
    sent(far_copy, 1, at_high, high)


def shards(nx, ny, ham, ovl, den, leaving, codes, slots):
    high, group = nx // LOW, LOW * ny
    vmem = pl.BlockSpec(memory_space=pltpu.VMEM)
    smem = pl.BlockSpec(memory_space=pltpu.SMEM)
    dma = pltpu.SemaphoreType.DMA
    purified, energy = pl.pallas_call(
        functools.partial(kernel, nx, ny),
        out_shape=(
            jax.ShapeDtypeStruct(den.shape, F32),
            jax.ShapeDtypeStruct((1,), F32),
        ),
        in_specs=[pl.BlockSpec(memory_space=pl.ANY)] * 6,
        out_specs=(vmem, smem),
        scratch_shapes=[
            *[pltpu.VMEM((TYPES, SIDE, COLUMNS), F32)] * 3,
            pltpu.SMEM((TYPES,), I32),
            pltpu.SMEM((TYPES, KEPT), I32),
            pltpu.SMEM((TYPES, KEPT), I32),
            pltpu.VMEM((3, 9 * TYPES, SIDE, COLUMNS), F32),
            pltpu.VMEM((TYPES, SIDE, COLUMNS), F32),
            pltpu.VMEM((TYPES, SIDE, COLUMNS), F32),
            pltpu.VMEM(((9 * TYPES + 1) * KEPT, SIDE, 128), BF16),
            pltpu.VMEM(((9 * TYPES + 1) * KEPT, SIDE, 128), BF16),
            pltpu.VMEM((2, TYPES, 2 * SIDE, COLUMNS), BF16),
            pltpu.VMEM((TYPES, SIDE, COLUMNS), F32),
            pltpu.VMEM((TYPES, SIDE, COLUMNS), F32),
            pltpu.VMEM((9, 8, 128), I32),
            pltpu.SMEM((9, 8, 128), I32),
            pltpu.VMEM((TYPES * KEPT, 128), I32),
            pltpu.SMEM((TYPES * KEPT, 128), I32),
            pltpu.VMEM((2, group, 1, 128), F32),
            pltpu.VMEM((2, high, 1, 128), F32),
            dma((3, 9 * TYPES)),
            dma((3, 9 * TYPES)),
            dma((TYPES,)),
            dma((TYPES,)),
            dma((9,)),
            dma((9,)),
            dma((2, 2, max(group, high))),
            dma((2, 2, max(group, high))),
            dma((2,)),
            dma((6,)),
        ],
        compiler_params=pltpu.CompilerParams(
            collective_id=0, has_side_effects=True, vmem_limit_bytes=60 * 1024 * 1024
        ),
    )(
        *(m.reshape(TYPES, SIDE, COLUMNS) for m in (ham, ovl, den)),
        leaving.reshape(TYPES), codes.reshape(TYPES, KEPT), slots.reshape(TYPES, KEPT),
    )
    return purified, energy.reshape(())


def solution(mesh):
    whole = P("gx", "gy", None, None, None)
    few = P("gx", "gy", None, None)
    return jax.shard_map(
        functools.partial(shards, mesh.shape["gx"], mesh.shape["gy"]),
        mesh=mesh,
        in_specs=(whole, whole, whole, few, few, few),
        out_specs=(whole, P()),
        check_vma=False,
    )
```

```python
import functools

import jax
import jax.numpy as jnp
from jax import lax
from jax.experimental import pallas as pl
from jax.experimental.pallas import tpu as pltpu
from jax.sharding import PartitionSpec as P

MESH = pl.DeviceIdType.MESH
F32, BF16, I32 = jnp.float32, jnp.bfloat16, jnp.int32
A, B, C, D = range(4)
SIDE, KEPT, TYPES = 64, 8, 4
COLUMNS = SIDE * KEPT
OVL, DEN, MIX = range(3)
BEHIND = (1, 0, 3, 2)
AROUND = [(ux, uy) for ux in (-1, 0, 1) for uy in (-1, 0, 1) if (ux, uy) != (0, 0)]
LOW = 4


def row_id(dx, dy, kind):
    return (3 * (dx + 1) + (dy + 1)) * TYPES + kind


def domain_key(code):
    across = (code * 11) >> 5
    return (across - 1) * 64 + (code - 3 * across - 1) * 8


def folded(tile):
    return jnp.sum(tile.reshape(tile.shape[0] // 8, 8, 128), axis=0)


def kernel(
    nx, ny,
    ham_hbm, ovl_hbm, den_hbm, leaving_hbm, codes_hbm, slots_hbm,
    out, energy,
    ham, ovl, den, leaving, codes, slots,
    rim, ham_out, ham_home, tiles_s, tiles_p, lhs, second, last,
    near, near_s, index_v, index_s, near_sums, far_sums,
    send_sem, recv_sem, ham_send, ham_recv, near_send, near_recv, sum_send, sum_recv, local_sem, load_sem,
):
    x, y = lax.axis_index("gx"), lax.axis_index("gy")
    high = nx // LOW
    group = LOW * ny
    at_high, at_low = x // LOW, (x % LOW) * ny + y

    def beside(ux, uy):
        return (lax.rem(x + ux + nx, nx), lax.rem(y + uy + ny, ny))

    def near_peer(j):
        return (at_high * LOW + j // ny, j % ny)

    def far_peer(j):
        return (j * LOW + x % LOW, y)

    loads = [
        pltpu.make_async_copy(there, here, load_sem.at[k])
        for k, (there, here) in enumerate((
            (leaving_hbm, leaving), (codes_hbm, codes), (slots_hbm, slots),
            (ovl_hbm, ovl), (den_hbm, den), (ham_hbm, ham),
        ))
    ]
    for load in loads:
        load.start()

    barrier = pltpu.get_barrier_semaphore()
    for ux, uy in AROUND:
        pl.semaphore_signal(barrier, inc=1, device_id=beside(ux, uy), device_id_type=MESH)

    def greet_near(o, carry):
        pl.semaphore_signal(barrier, inc=1, device_id=near_peer((at_low + o) % group), device_id_type=MESH)
        return carry

    def greet_far(o, carry):
        pl.semaphore_signal(barrier, inc=1, device_id=far_peer((at_high + o) % high), device_id_type=MESH)
        return carry

    lax.fori_loop(1, group, greet_near, 0)
    lax.fori_loop(1, high, greet_far, 0)

    lane = lax.broadcasted_iota(I32, (8, 128), 1)
    sub = lax.broadcasted_iota(I32, (8, 128), 0)

    for load in loads[:3]:
        load.wait()
    note = jnp.zeros((8, 128), I32)
    for kind in range(TYPES):
        slot = leaving[BEHIND[kind]]
        for c in range(KEPT):
            key = domain_key(codes[slot, c]) + slots[slot, c]
            note = jnp.where((sub == kind) & (lane == c), key, note)
        note = jnp.where((sub == TYPES) & (lane == slot), kind, note)
    near[4] = note

    for load in loads[3:5]:
        load.wait()
    start = jnp.zeros((8, 128), F32)
    for kind in range(TYPES):
        slot = leaving[kind]
        mine = row_id(*((1, 0), (-1, 0), (0, 1), (0, -1))[kind], kind)
        s_row, p_row = ovl[slot], den[slot]
        rim[OVL, mine] = s_row
        rim[DEN, mine] = p_row
        prod = s_row * p_row
        for k in range(COLUMNS // 128):
            start += folded(prod[:, k * 128 : (k + 1) * 128])

    pl.semaphore_wait(barrier, len(AROUND) + group - 1 + high - 1)

    def row_copy(m, which, there, ux, uy, left=None):
        return pltpu.make_async_remote_copy(
            src_ref=rim.at[m, which],
            dst_ref=rim.at[m, there],
            send_sem=send_sem.at[m, there if left is None else left],
            recv_sem=recv_sem.at[m, there],
            device_id=beside(ux, uy),
            device_id_type=MESH,
        )

    def send(m, dx, dy, kind, ux, uy):
        row_copy(m, row_id(dx, dy, kind), row_id(dx - ux, dy - uy, kind), ux, uy).start()

    def landed(m, which):
        row_copy(m, which, which, 1, 0).wait_recv()

    def arrive(m, dx, dy, kind):
        landed(m, row_id(dx, dy, kind))

    core = lax.rem(x, 2)
    outer, inner = 2 * core - 1, 1 - 2 * core
    outer_ids, inner_ids = core * (6 * TYPES), (1 - core) * (6 * TYPES)

    def outer_id(dy, kind):
        return outer_ids + ((dy + 1) * TYPES + kind)

    def send_inner(m, dy, kind):
        left = inner_ids + ((dy + 1) * TYPES + kind)
        row_copy(m, row_id(0, dy, kind), outer_id(dy, kind), inner, 0, left).start()

    def outer_on(m, dy, kind, uy):
        landed(m, outer_id(dy, kind))
        row_copy(m, outer_id(dy, kind), outer_id(dy - uy, kind), 0, uy).start()

    def start_y(m):
        send(m, 0, 1, C, 0, 1)
        send(m, 0, -1, D, 0, -1)
        for u in (1, -1):
            send(m, 1, 0, A, 0, u)
            send(m, -1, 0, B, 0, u)

    def start_x(m):
        send(m, 1, 0, A, 1, 0)
        send(m, -1, 0, B, -1, 0)
        for u in (1, -1):
            send(m, 0, 1, C, u, 0)
            send(m, 0, -1, D, u, 0)

    near_copies = []

    def tell_pattern():
        for k, (ux, uy) in enumerate(AROUND):
            there = row_id(-ux, -uy, 0) // TYPES
            copy = pltpu.make_async_remote_copy(
                src_ref=near.at[4],
                dst_ref=near.at[there],
                send_sem=near_send.at[there],
                recv_sem=near_recv.at[there],
                device_id=beside(ux, uy),
                device_id_type=MESH,
            )
            copy.start()
            near_copies.append(copy)

    tell_pattern()
    start_x(OVL)
    start_y(OVL)
    start_x(DEN)

    def first_tier(m):
        for kind, uy in ((C, 1), (D, -1)):
            arrive(m, 0, 0, kind)
            send(m, 0, 0, kind, 0, uy)
            if m == OVL:
                for u in (1, -1):
                    send(m, 0, 0, kind, u, 0)
            else:
                send_inner(m, 0, kind)
        arrive(m, 0, 0, A)
        send(m, 0, 0, A, 1, 0)
        arrive(m, 0, 0, B)
        send(m, 0, 0, B, -1, 0)
        for u in (1, -1):
            arrive(m, 1, u, A)
            send(m, 1, u, A, 1, 0)
            arrive(m, -1, u, B)
            send(m, -1, u, B, -1, 0)
        if m == DEN:
            outer_on(m, 0, C, 1)
            outer_on(m, 0, D, -1)

    def second_tier(m):
        for kind, uy in ((C, 1), (D, -1)):
            arrive(m, 0, -uy, kind)
            if m == OVL:
                for u in (1, -1):
                    send(m, 0, -uy, kind, u, 0)
            else:
                send_inner(m, -uy, kind)
        for u in (1, -1):
            arrive(m, 0, u, A)
            send(m, 0, u, A, 1, 0)
            arrive(m, 0, u, B)
            send(m, 0, u, B, -1, 0)

    half = lax.broadcasted_iota(I32, (SIDE, 128), 1) < SIDE

    def split_row(m, which, tiles, scale=None):
        for pair in range(KEPT // 2):
            v = rim[m, which, :, pair * 128 : (pair + 1) * 128]
            if scale is not None:
                v = v * scale
            top = v.astype(BF16)
            rest = pltpu.roll((v - top.astype(F32)).astype(BF16), SIDE, 1)
            tiles[(which + 1) * KEPT + 2 * pair] = jnp.where(half, top, rest)
            tiles[(which + 1) * KEPT + 2 * pair + 1] = jnp.where(half, rest, top)

    def split_left(into, i, columns, v):
        top = v.astype(BF16)
        lhs[into, i, 0:SIDE, columns] = top
        lhs[into, i, SIDE : 2 * SIDE, columns] = (v - top.astype(F32)).astype(BF16)

    def left_rows(m, scale=None):
        for i in range(TYPES):
            v = rim[m, row_id(0, 0, i)]
            split_left(0, i, slice(None), v if scale is None else v * scale)

    wide = lax.broadcasted_iota(I32, (SIDE, 128), 1) < SIDE

    def row_product(left, tiles, i, emit, carry=0):
        a = lhs[left, i]
        for pair in range(KEPT // 2):
            right = jnp.concatenate(
                [
                    jnp.concatenate([tiles[index_s[i * KEPT + b, e]] for e in range(KEPT)], axis=0)
                    for b in (2 * pair, 2 * pair + 1)
                ],
                axis=1,
            )
            full = jnp.dot(a, right, preferred_element_type=F32)
            both = full[:SIDE] + full[SIDE:]
            even, odd = both[:, :128], both[:, 128:]
            even = even + pltpu.roll(even, SIDE, 1)
            odd = odd + pltpu.roll(odd, SIDE, 1)
            carry = emit(i, slice(pair * 128, (pair + 1) * 128), jnp.where(wide, even, odd), carry)
        return carry

    def product(left, tiles, emit, carry=0):
        return lax.fori_loop(0, TYPES, lambda i, carry: row_product(left, tiles, i, emit, carry), carry, unroll=True)

    def to_left(into):
        def emit(i, columns, v, carry):
            split_left(into, i, columns, v)
            return carry

        return emit

    def to_left_and_second(into):
        def emit(i, columns, v, carry):
            split_left(into, i, columns, v)
            second[i, :, columns] = v
            return carry

        return emit

    own = row_id(0, 0, 0)

    for k in range(KEPT):
        tiles_s[k] = jnp.zeros((SIDE, 128), BF16)
        tiles_p[k] = jnp.zeros((SIDE, 128), BF16)
    first_tier(OVL)
    start_y(DEN)
    outer_on(DEN, 1, C, 1)
    outer_on(DEN, -1, D, -1)

    for copy in near_copies:
        copy.wait_recv()
    to_scalars = pltpu.make_async_copy(near, near_s, local_sem.at[0])
    to_scalars.start()
    to_scalars.wait()

    for kind in range(TYPES):
        slot = leaving[BEHIND[kind]]
        mine = jnp.zeros((8, 128), I32)
        for b in range(KEPT):
            mine = jnp.where(sub == b, domain_key(codes[slot, b]) + slots[slot, b], mine)
        found = jnp.zeros((8, 128), I32)
        for a in range(KEPT):
            code = codes[slot, a]
            what = near_s[code, TYPES, slots[slot, a]]
            keys = near[code, pl.ds(what, 1), :] + domain_key(code)
            hit = (keys == mine) & (lane < KEPT)
            tile = jnp.where(hit, (code * TYPES + what + 1) * KEPT + lane, 0)
            found = jnp.where(lane == a, jnp.sum(tile, axis=1, keepdims=True), found)
        index_v[kind * KEPT : (kind + 1) * KEPT, :] = found
    to_scalars = pltpu.make_async_copy(index_v, index_s, local_sem.at[1])
    to_scalars.start()
    to_scalars.wait()

    second_tier(OVL)
    first_tier(DEN)
    left_rows(DEN)

    def middle(m, tiles):
        def one(j, carry):
            split_row(m, row_id(0, -1, 0) + j, tiles)
            return carry

        def sides(j, carry):
            split_row(m, row_id(1, -1, A) + j * TYPES, tiles)
            split_row(m, row_id(-1, -1, B) + j * TYPES, tiles)
            return carry

        lax.fori_loop(0, 3 * TYPES, one, 0)
        lax.fori_loop(0, 3, sides, 0)

    def third_tier(m, tiles):
        def one(j, carry):
            skip = lax.rem(j + 1, 3) * TYPES
            if m == DEN:
                for kind in (C, D):
                    landed(m, inner_ids + kind + skip)

                @pl.when(j == 1)
                def _():
                    landed(m, outer_id(1, D))

                @pl.when(j == 2)
                def _():
                    landed(m, outer_id(-1, C))

            for u, kinds in ((1, (B, C, D)), (-1, (A, C, D))):
                for kind in kinds:
                    which = row_id(u, -1, kind) + skip
                    if m == OVL or kind < C:
                        landed(m, which)
                    split_row(m, which, tiles)
            return carry

        lax.fori_loop(0, 3, one, 0)

    middle(OVL, tiles_s)
    third_tier(OVL, tiles_s)
    second_tier(DEN)

    ham_copies = []
    loads[5].wait()
    for kind in range(TYPES):
        ham_out[kind] = ham[leaving[kind]]
    for kind, (ux, uy) in enumerate(((1, 0), (-1, 0), (0, 1), (0, -1))):
        copy = pltpu.make_async_remote_copy(
            src_ref=ham_out.at[kind],
            dst_ref=ham_home.at[kind],
            send_sem=ham_send.at[kind],
            recv_sem=ham_recv.at[kind],
            device_id=beside(ux, uy),
            device_id_type=MESH,
        )
        copy.start()
        ham_copies.append(copy)

    product(0, tiles_s, to_left(1))
    middle(DEN, tiles_p)
    third_tier(DEN, tiles_p)

    def mixed_out(i, columns, v, total):
        m = 3.0 * second[i, :, columns] - 2.0 * v
        rim[MIX, own + i, :, columns] = m
        return total + folded(m * rim[OVL, own + i, :, columns])

    def mixed_along_y(i):
        for u in (1, -1):
            row_copy(MIX, own + i, row_id(0, -u, 0) + i, 0, u).start()

    def mixed_sent(i):
        for u in (1, -1):
            row_copy(MIX, own + i, row_id(-u, 0, 0) + i, u, 0).start()

        @pl.when(i < 2)
        def _():
            mixed_along_y(i)

    def one_row(i, total):
        row_product(1, tiles_p, i, to_left_and_second(0))
        row_product(0, tiles_s, i, to_left(1))
        total = row_product(1, tiles_p, i, mixed_out, total)
        mixed_sent(i)
        return total

    count = lax.fori_loop(0, TYPES, one_row, jnp.zeros((8, 128), F32))

    def near_copy(s, j, mine):
        return pltpu.make_async_remote_copy(
            src_ref=near_sums.at[s, at_low],
            dst_ref=near_sums.at[s, mine],
            send_sem=sum_send.at[s, 0, j],
            recv_sem=sum_recv.at[s, 0, mine],
            device_id=near_peer(j),
            device_id_type=MESH,
        )

    def far_copy(s, j, mine):
        return pltpu.make_async_remote_copy(
            src_ref=far_sums.at[s, at_high],
            dst_ref=far_sums.at[s, mine],
            send_sem=sum_send.at[s, 1, j],
            recv_sem=sum_recv.at[s, 1, mine],
            device_id=far_peer(j),
            device_id_type=MESH,
        )

    def spread(copy_of, s, me, members):
        def step(o, carry):
            copy_of(s, (me + o) % members, me).start()
            return carry

        lax.fori_loop(1, members, step, 0, unroll=True)

    def collect(copy_of, s, me, members):
        def step(o, carry):
            j = (me + o) % members
            copy_of(s, j, j).wait_recv()
            return carry

        lax.fori_loop(1, members, step, 0, unroll=True)

    def sent(copy_of, s, me, members):
        def step(o, carry):
            copy_of(s, (me + o) % members, me).wait_send()
            return carry

        lax.fori_loop(1, members, step, 0)

    across = lax.broadcasted_iota(I32, (1, 128), 1)

    def over_all(tile):
        return jnp.sum(jnp.sum(tile, axis=0, keepdims=True), axis=1, keepdims=True)

    near_sums[0, at_low] = jnp.where(across < SIDE, over_all(start), over_all(count))
    spread(near_copy, 0, at_low, group)

    def pass_on(i):
        for dy in (-1, 1):
            arrive(MIX, 0, dy, i)
            for u in (1, -1):
                send(MIX, 0, dy, i, u, 0)

    pass_on(0)
    mixed_along_y(2)
    collect(near_copy, 0, at_low, group)
    far_sums[0, at_high] = jnp.sum(near_sums[0], axis=0)
    spread(far_copy, 0, at_high, high)
    pass_on(1)
    mixed_along_y(3)
    pass_on(2)
    for u in (1, -1):
        if u == 1:
            landed(MIX, outer_id(0, 3))
        row_copy(MIX, outer_id(0, 3), outer_id(-u, 3), 0, u).start()
    collect(far_copy, 0, at_high, high)
    counts = jnp.sum(far_sums[0], axis=0)
    count_start = counts[:, :1]
    scale = count_start / counts[:, SIDE : SIDE + 1]
    left_rows(MIX, scale)
    for dy in (-1, 1):
        arrive(MIX, 0, dy, 3)
        send_inner(MIX, dy, 3)
    product(0, tiles_s, to_left(1))

    def mixed_middle(j, carry):
        split_row(MIX, row_id(0, -1, 0) + j, tiles_p, scale)
        return carry

    def mixed_sides(j, carry):
        skip = lax.rem(j + 1, 3) * TYPES
        landed(MIX, inner_ids + 3 + skip)

        @pl.when(j > 0)
        def _():
            landed(MIX, outer_ids + 3 + skip)

        for kind in range(TYPES):
            for u in (1, -1):
                which = row_id(u, -1, kind) + skip
                if kind < 3:
                    landed(MIX, which)
                split_row(MIX, which, tiles_p, scale)
        return carry

    lax.fori_loop(0, 3 * TYPES, mixed_middle, 0, unroll=3)
    lax.fori_loop(0, 3, mixed_sides, 0, unroll=True)
    product(1, tiles_p, to_left_and_second(0))
    product(0, tiles_s, to_left(1))

    def last_out(i, columns, v, carry):
        total, largest = carry
        m = 3.0 * second[i, :, columns] - 2.0 * v
        last[i, :, columns] = m
        return (
            total + folded(m * rim[OVL, own + i, :, columns]),
            jnp.maximum(largest, jnp.max(jnp.abs(m).reshape(SIDE // 8, 8, 128), axis=0)),
        )

    zero = jnp.zeros((8, 128), F32)
    count, largest = product(1, tiles_p, last_out, (zero, zero))
    for copy in ham_copies:
        copy.wait_recv()
    largest = jnp.max(jnp.max(largest, axis=1, keepdims=True), axis=0, keepdims=True)
    size = jnp.where(largest > 1e-37, jnp.minimum(largest, 1e37), 1.0)
    inverse = 1.0 / size
    band = zero
    for i in range(TYPES):
        for k in range(COLUMNS // 128):
            columns = slice(k * 128, (k + 1) * 128)
            band += folded((last[i, :, columns] * inverse) * ham_home[i, :, columns])

    def joined(sums):
        biggest = jnp.max(sums, axis=0)
        ratio = pltpu.roll(sums, SIDE, 2) / pltpu.roll(biggest, SIDE, 1)[None]
        added = jnp.sum(jnp.where((across >= 32)[None], sums * ratio, sums), axis=0)
        return jnp.where(across < SIDE, added, biggest)

    near_sums[1, at_low] = jnp.where(
        across < 32, over_all(count), jnp.where(across < SIDE, over_all(band), size)
    )
    spread(near_copy, 1, at_low, group)
    for copy in (*near_copies, *ham_copies):
        copy.wait_send()

    first = {OVL: (row_id(1, 0, A), row_id(-1, 0, B), row_id(0, 1, C), row_id(0, -1, D))}
    first[DEN], first[MIX] = first[OVL], tuple(own + i for i in range(TYPES))
    for m in (OVL, DEN, MIX):
        for which in range(9 * TYPES):
            if which not in first[m]:
                row_copy(m, which, which, 1, 0).wait_send()
    sent(near_copy, 0, at_low, group)
    sent(far_copy, 0, at_high, high)
    sent(near_copy, 1, at_low, group)
    collect(near_copy, 1, at_low, group)
    far_sums[1, at_high] = joined(near_sums[1])
    spread(far_copy, 1, at_high, high)
    collect(far_copy, 1, at_high, high)
    sums = joined(far_sums[1])
    scale = count_start / sums[:, :1]
    for slot in range(TYPES):
        out[0, 0, slot] = scale * last[near_s[4, TYPES, slot]]
    basis = nx * ny * TYPES * SIDE
    energy[0] = jnp.sum(sums[:, 32:33] * (sums[:, SIDE : SIDE + 1] * scale)) / basis

    sent(far_copy, 1, at_high, high)


def shards(nx, ny, ham, ovl, den, leaving, codes, slots):
    high, group = nx // LOW, LOW * ny
    vmem = pl.BlockSpec(memory_space=pltpu.VMEM)
    smem = pl.BlockSpec(memory_space=pltpu.SMEM)
    dma = pltpu.SemaphoreType.DMA
    purified, energy = pl.pallas_call(
        functools.partial(kernel, nx, ny),
        out_shape=(
            jax.ShapeDtypeStruct(den.shape, F32),
            jax.ShapeDtypeStruct((1,), F32),
        ),
        in_specs=[pl.BlockSpec(memory_space=pl.ANY)] * 6,
        out_specs=(vmem, smem),
        scratch_shapes=[
            *[pltpu.VMEM((TYPES, SIDE, COLUMNS), F32)] * 3,
            pltpu.SMEM((TYPES,), I32),
            pltpu.SMEM((TYPES, KEPT), I32),
            pltpu.SMEM((TYPES, KEPT), I32),
            pltpu.VMEM((3, 9 * TYPES, SIDE, COLUMNS), F32),
            pltpu.VMEM((TYPES, SIDE, COLUMNS), F32),
            pltpu.VMEM((TYPES, SIDE, COLUMNS), F32),
            pltpu.VMEM(((9 * TYPES + 1) * KEPT, SIDE, 128), BF16),
            pltpu.VMEM(((9 * TYPES + 1) * KEPT, SIDE, 128), BF16),
            pltpu.VMEM((2, TYPES, 2 * SIDE, COLUMNS), BF16),
            pltpu.VMEM((TYPES, SIDE, COLUMNS), F32),
            pltpu.VMEM((TYPES, SIDE, COLUMNS), F32),
            pltpu.VMEM((9, 8, 128), I32),
            pltpu.SMEM((9, 8, 128), I32),
            pltpu.VMEM((TYPES * KEPT, 128), I32),
            pltpu.SMEM((TYPES * KEPT, 128), I32),
            pltpu.VMEM((2, group, 1, 128), F32),
            pltpu.VMEM((2, high, 1, 128), F32),
            dma((3, 9 * TYPES)),
            dma((3, 9 * TYPES)),
            dma((TYPES,)),
            dma((TYPES,)),
            dma((9,)),
            dma((9,)),
            dma((2, 2, max(group, high))),
            dma((2, 2, max(group, high))),
            dma((2,)),
            dma((6,)),
        ],
        compiler_params=pltpu.CompilerParams(
            collective_id=0, has_side_effects=True, vmem_limit_bytes=60 * 1024 * 1024
        ),
    )(
        *(m.reshape(TYPES, SIDE, COLUMNS) for m in (ham, ovl, den)),
        leaving.reshape(TYPES), codes.reshape(TYPES, KEPT), slots.reshape(TYPES, KEPT),
    )
    return purified, energy.reshape(())


def solution(mesh):
    whole = P("gx", "gy", None, None, None)
    few = P("gx", "gy", None, None)
    return jax.shard_map(
        functools.partial(shards, mesh.shape["gx"], mesh.shape["gy"]),
        mesh=mesh,
        in_specs=(whole, whole, whole, few, few, few),
        out_specs=(whole, P()),
        check_vma=False,
    )
```
